32 devices in a mesh: angle: 4 (over z), slab: 4 (over x, core), tile: 2 (over y).
Axes of the slice: x: 2, y: 2, z: 4, core: 2. Of those that a mesh axis runs over, the one named last changes fastest.
Arguments:
- volume: bfloat16 [2, 4, 384, 1536], P(None, 'slab', 'tile'), may hold values from -2 to 2
- probe_wave: float32 [2, 256, 256], replicated, may hold values from -6 to 6
- amplitudes: bfloat16 [4, 2, 4, 2, 256, 256], P('angle', 'tile', 'slab'), may hold values from 0.099609375 to 3
- offsets: int32 [4, 2, 4, 2], P('angle', 'tile', 'slab'), may hold values from 0 to 128
- column_starts: int32 [4, 2, 4, 2], P('angle', 'tile', 'slab'), may hold values from 0 to 1280
- counts: int32 [4, 2, 4], P('angle', 'tile', 'slab'), may hold values from 1 to 2, as said below
- angle_ids: int32 [4], P('angle'), may hold values from 0 to 1199
Outputs:
- new_volume: float32 [2, 4, 384, 1536], P(None, 'slab', 'tile')
The draws below stay inside these ranges and needn't reach their ends.
Inputs may be any that keep to these rules, and one draw needn't show every extreme that they name: counts gives the live slots of one device; slots at or beyond it are ignored; in every draw some device has 2.
All inputs are finite; a program needn't handle non-finite values.
Results may differ from the reference program's by a relative error of at most 0.04.
Values may be sent and summed in bfloat16 or wider, within the bound.
A program may use at most 64 MiB of HBM per device.

```python
import math
import jax
import jax.numpy as jnp
from jax import lax

PATCH = 256
COLS = 1536
TILE_ROWS = 192
POS_CAP = 2
ANGLES = 4
TILES = 2
SLABS = 4
DEPTH = 4
ROWS = 384


def draw_counts(key, part):
    key = jax.random.fold_in(key, 7)
    uniform_draw = jax.random.randint(key, (ANGLES, TILES, SLABS), 0, POS_CAP)
    live_count = 1 + uniform_draw * uniform_draw // POS_CAP
    return live_count.at[0, 0, 0].set(POS_CAP).astype(jnp.int32)


def with_ends(values, stream_key, least, largest):
    longest = values.shape.index(max(values.shape))
    spots = []
    for shift in (0, 1):
        where = [jax.random.randint(jax.random.fold_in(stream_key, axis), (), 0, length) for axis, length in enumerate(values.shape)]
        where[longest] = (where[longest] + shift) % values.shape[longest]
        spots.append(tuple(where))
    return values.at[spots[0]].set(least).at[spots[1]].set(largest)


def shard_levels(rng, dims, cuts, smallest, high):
    def one(position, parts):
        steps = jax.random.uniform(jax.random.fold_in(jax.random.fold_in(rng, 6), position), (parts,), jnp.float32, smallest / len(cuts), high / len(cuts))
        return jnp.repeat(jnp.exp(steps), dims[position] // parts).reshape((-1,) + (1,) * (len(dims) - position - 1))

    level = one(*cuts[0])
    for cut in cuts[1:]:
        level = level * one(*cut)
    return level


def centred(key, extent, spread, bound, cuts=(), held_as=jnp.bfloat16):
    values = jax.random.normal(key, extent, jnp.float32) * spread
    if len(cuts) > 0:
        values = shard_levels(key, extent, cuts, -0.22, 0.18) * values
    return jnp.clip(values, min=-bound, max=bound).astype(held_as)


def setup_inputs(seed: int = 0) -> dict:
    seeds = jax.random.split(jax.random.key(seed), 8)
    return {
        "volume": centred(seeds[0], (2, DEPTH, ROWS, COLS), 0.25, 2.0, ((1, 4), (2, 2))),
        "probe_wave": centred(seeds[1], (2, PATCH, PATCH), 1.0, 6.0, (), jnp.float32),
        "amplitudes": jnp.clip(jnp.exp(math.log(3.0) - 3.4051113 * jax.random.uniform(seeds[2], (ANGLES, TILES, SLABS, POS_CAP, PATCH, PATCH), jnp.float32) ** shard_levels(seeds[2], (ANGLES, TILES, SLABS, POS_CAP, PATCH, PATCH), ((0, 4), (1, 2), (2, 4)), -0.2, 0.2)), 0.099609375, 3.0).astype(jnp.bfloat16),
        "offsets": with_ends(jax.random.randint(seeds[3], (ANGLES, TILES, SLABS, POS_CAP), 0, min(TILE_ROWS, 2 * TILE_ROWS - PATCH + 1)), jax.random.fold_in(seeds[3], 1), 0, (min(TILE_ROWS, 2 * TILE_ROWS - PATCH + 1)) - 1).astype(jnp.int32),
        "column_starts": with_ends(jax.random.randint(seeds[4], (ANGLES, TILES, SLABS, POS_CAP), 0, COLS - PATCH + 1), jax.random.fold_in(seeds[4], 1), 0, COLS - PATCH).astype(jnp.int32),
        "counts": draw_counts(jax.random.fold_in(seeds[7], 71), 0),
        "angle_ids": with_ends(jax.random.randint(seeds[6], (ANGLES,), 0, 1200), jax.random.fold_in(seeds[6], 1), 0, 1199).astype(jnp.int32),
    }


angle_center = 600
shear_divisor = 64
step_size = 0.03
floor_square = 0.25

def dft_tables(plane_width):
    index_line = jnp.arange(plane_width, dtype=jnp.int32)
    product_mod = jnp.mod(index_line[:, None] * index_line[None, :], plane_width)
    phase_table = product_mod.astype(jnp.float32) * (2.0 * 3.141592653589793 / plane_width)
    scale_factor = plane_width ** (-0.5)
    table_real = (jnp.cos(phase_table) * scale_factor).astype(jnp.bfloat16)
    table_imag = (-jnp.sin(phase_table) * scale_factor).astype(jnp.bfloat16)
    return (table_real, table_imag)

def shear_shifts(angle_value, first_layer, layer_count, total_depth, column_count):
    layer_index = first_layer + jnp.arange(layer_count, dtype=jnp.int32)
    offset_layer = layer_index - total_depth // 2
    sheared = jnp.floor_divide((angle_value - angle_center) * offset_layer, shear_divisor)
    return jnp.mod(sheared, column_count).astype(jnp.int32)

def twodot(left_matrix, right_matrix):
    return jnp.dot(left_matrix, right_matrix, preferred_element_type=jnp.float32)

def patch_gradient(window, probe_wave, pattern, table_real, table_imag):
    window_wide = window.astype(jnp.float32)
    trans_mag = jnp.exp(-window_wide[1])
    trans_real = trans_mag * jnp.cos(window_wide[0])
    trans_imag = trans_mag * jnp.sin(window_wide[0])
    wave_real = (probe_wave[0] * trans_real - probe_wave[1] * trans_imag).astype(jnp.bfloat16)
    wave_imag = (probe_wave[0] * trans_imag + probe_wave[1] * trans_real).astype(jnp.bfloat16)
    left_real = (twodot(table_real, wave_real) - twodot(table_imag, wave_imag)).astype(jnp.bfloat16)
    left_imag = (twodot(table_real, wave_imag) + twodot(table_imag, wave_real)).astype(jnp.bfloat16)
    far_real = twodot(left_real, table_real) - twodot(left_imag, table_imag)
    far_imag = twodot(left_real, table_imag) + twodot(left_imag, table_real)
    ratio = pattern.astype(jnp.float32) / jnp.sqrt(far_real * far_real + far_imag * far_imag + floor_square)
    keeping = 1.0 - ratio
    resid_real = (far_real * keeping).astype(jnp.bfloat16)
    resid_imag = (far_imag * keeping).astype(jnp.bfloat16)
    back_real = (twodot(table_real, resid_real) + twodot(table_imag, resid_imag)).astype(jnp.bfloat16)
    back_imag = (twodot(table_real, resid_imag) - twodot(table_imag, resid_real)).astype(jnp.bfloat16)
    exit_real = twodot(back_real, table_real) + twodot(back_imag, table_imag)
    exit_imag = twodot(back_imag, table_real) - twodot(back_real, table_imag)
    mixed_real = probe_wave[0] * exit_real + probe_wave[1] * exit_imag
    mixed_imag = probe_wave[0] * exit_imag - probe_wave[1] * exit_real
    final_real = trans_real * mixed_real + trans_imag * mixed_imag
    final_imag = trans_real * mixed_imag - trans_imag * mixed_real
    return jnp.stack([final_imag, -final_real])

def slot_update(buffer, extended, start_row, start_column, pattern, probe_wave, table_real, table_imag):
    plane_width = pattern.shape[-1]
    zero_index = jnp.zeros((), jnp.int32)
    corner = (zero_index, start_row.astype(jnp.int32), start_column.astype(jnp.int32))
    window = lax.dynamic_slice(extended, corner, (2, plane_width, plane_width))
    gradient = patch_gradient(window, probe_wave, pattern, table_real, table_imag)
    previous = lax.dynamic_slice(buffer, corner, (2, plane_width, plane_width))
    return lax.dynamic_update_slice(buffer, previous + gradient, corner)

def keep_buffer(buffer):
    return buffer

def reference(volume, probe_wave, amplitudes, offsets, column_starts, counts, angle_ids):
    total_depth = volume.shape[1]
    row_count = volume.shape[2]
    column_count = volume.shape[3]
    plane_width = amplitudes.shape[-1]
    tile_count = counts.shape[1]
    slab_count = counts.shape[2]
    capacity = offsets.shape[3]
    tile_rows = row_count // tile_count
    layer_count = total_depth // slab_count
    slot_total = tile_count * capacity
    table_real, table_imag = dft_tables(plane_width)

    def one_angle(gradient_sum, inputs):
        angle_value, patterns, row_starts, col_starts, live_counts = inputs
        shifts = shear_shifts(angle_value, 0, total_depth, total_depth, column_count)

        def slab_partial(slab_index):

            def add_layer(running, within):
                layer_index = slab_index * layer_count + within
                layer_field = lax.dynamic_index_in_dim(volume, layer_index, 1, keepdims=False)
                rolled = jnp.roll(layer_field, -shifts[layer_index], axis=-1)
                return (running + rolled.astype(jnp.float32), None)
            partial_value, _ = lax.scan(add_layer, jnp.zeros((2, row_count, column_count), jnp.float32), jnp.arange(layer_count, dtype=jnp.int32))
            return partial_value.astype(jnp.bfloat16)

        def add_partial(running, slab_index):
            return (running + slab_partial(slab_index).astype(jnp.float32), None)
        projection_wide, _ = lax.scan(add_partial, jnp.zeros((2, row_count, column_count), jnp.float32), jnp.arange(slab_count, dtype=jnp.int32))
        projection = projection_wide.astype(jnp.bfloat16)
        extended = jnp.concatenate([projection, jnp.zeros((2, tile_rows, column_count), jnp.bfloat16)], axis=1)

        def one_slab(plane_sum, slab_index):
            slab_patterns = lax.dynamic_index_in_dim(patterns, slab_index, 1, keepdims=False)
            slab_patterns = slab_patterns.reshape(slot_total, plane_width, plane_width)
            slab_rows = lax.dynamic_index_in_dim(row_starts, slab_index, 1, keepdims=False).reshape(slot_total)
            slab_cols = lax.dynamic_index_in_dim(col_starts, slab_index, 1, keepdims=False).reshape(slot_total)
            slab_live = lax.dynamic_index_in_dim(live_counts, slab_index, 1, keepdims=False)

            def one_slot(buffer, slot_index):
                tile_index = slot_index // capacity
                within = slot_index % capacity
                is_live = within < slab_live[tile_index]
                start_row = (tile_index * tile_rows + slab_rows[slot_index]).astype(jnp.int32)

                def add_patch(current):
                    return slot_update(current, extended, start_row, slab_cols[slot_index], slab_patterns[slot_index], probe_wave, table_real, table_imag)
                return (lax.cond(is_live, add_patch, keep_buffer, buffer), None)
            buffer, _ = lax.scan(one_slot, jnp.zeros(extended.shape, jnp.float32), jnp.arange(slot_total, dtype=jnp.int32))
            rounded = buffer[:, :row_count].astype(jnp.bfloat16)
            return (plane_sum + rounded.astype(jnp.float32), None)
        plane_gradient, _ = lax.scan(one_slab, jnp.zeros((2, row_count, column_count), jnp.float32), jnp.arange(slab_count, dtype=jnp.int32))
        layer_gradient = jax.vmap(lambda amount: jnp.roll(plane_gradient, amount, axis=-1))(shifts)
        return (gradient_sum + jnp.moveaxis(layer_gradient, 0, 1), None)
    gradient_sum, _ = lax.scan(one_angle, jnp.zeros(volume.shape, jnp.float32), (angle_ids, amplitudes, offsets, column_starts, counts))
    return volume.astype(jnp.float32) - step_size * gradient_sum
```

```python
import functools

import jax
import jax.numpy as jnp
import numpy as np
from jax import lax
from jax.experimental import pallas as pl
from jax.experimental.pallas import tpu as pltpu
from jax.sharding import PartitionSpec as P

MESH = pl.DeviceIdType.MESH
BF16 = jnp.bfloat16
F32 = jnp.float32
MIB = 1024 * 1024

angle_center = 600
shear_divisor = 64
step_size = 0.03
floor_square = 0.25
row_chunks = 4


def dft_tables(width):
    line = np.arange(width)
    phase = ((line[:, None] * line[None, :]) % width) * (2.0 * np.pi / width)
    scale = width ** (-0.5)
    return (
        jnp.asarray((np.cos(phase) * scale).astype(np.float32), BF16),
        jnp.asarray((-np.sin(phase) * scale).astype(np.float32), BF16),
    )


def wrapped_shift(angle_value, layer, depth, columns):
    sheared = jnp.right_shift((angle_value - angle_center) * (layer - depth // 2), 6)
    rest = lax.rem(sheared, jnp.int32(columns))
    return jnp.where(rest < 0, rest + columns, rest)


def remote(src, dst, send, recv, axis, index):
    return pltpu.make_async_remote_copy(
        src_ref=src, dst_ref=dst, send_sem=send, recv_sem=recv,
        device_id={axis: index}, device_id_type=MESH,
    )


def slab_partners():
    slab = lax.axis_index("slab")
    core = slab % 2
    side = slab // 2
    return core, side, slab + 1 - 2 * core, slab + 2 - 4 * side


def greet(barrier, axis, index, here):
    @pl.when(here)
    def _():
        pl.semaphore_signal(barrier, inc=1, device_id={axis: index}, device_id_type=MESH)


def project_kernel(
    tiles, angles, rolled, ids, ext, all_ids,
    near, half, far, s1, r1, s2, r2, s3, r3, s4, r4, s5, r5, s6, r6, local_sem,
):
    rows = rolled.shape[1]
    size = rows // row_chunks
    core, side, mate, other = slab_partners()
    tile = lax.axis_index("tile")
    angle = lax.axis_index("angle")

    barrier = pltpu.get_barrier_semaphore()
    pl.semaphore_signal(barrier, inc=1, device_id={"slab": mate}, device_id_type=MESH)
    pl.semaphore_signal(barrier, inc=1, device_id={"slab": other}, device_id_type=MESH)
    for step in range(1, angles):
        pl.semaphore_signal(
            barrier, inc=1, device_id={"angle": (angle + step) % angles}, device_id_type=MESH
        )
    greet(barrier, "tile", tile - 1, tile > 0)
    greet(barrier, "tile", tile + 1, tile < tiles - 1)
    peers = (tile > 0).astype(jnp.int32) + (tile < tiles - 1).astype(jnp.int32)
    pl.semaphore_wait(barrier, 1 + angles + peers)

    def part(k, base=0):
        return pl.ds(base + k * size, size)

    first = [
        remote(rolled.at[1 - core, part(k)], near.at[part(k)], s1.at[k], r1.at[k], "slab", mate)
        for k in range(row_chunks)
    ]
    for copy in first:
        copy.start()
    id_copies = [
        remote(ids, all_ids.at[angle], s6.at[step], r6.at[step], "angle", (angle + step) % angles)
        for step in range(1, angles)
    ]
    for copy in id_copies:
        copy.start()
    own_ids = pltpu.make_async_copy(ids, all_ids.at[angle], local_sem)
    own_ids.start()

    second = []
    for k in range(row_chunks):
        first[k].wait_recv()
        half[part(k)] = (
            rolled[core, part(k)].astype(F32) + near[part(k)].astype(F32)
        ).astype(BF16)
        second.append(remote(half.at[part(k)], far.at[part(k)], s2.at[k], r2.at[k], "slab", other))
        second[k].start()

    third, down = [], []
    for k in range(row_chunks):
        second[k].wait_recv()
        ext[core, part(k)] = (half[part(k)].astype(F32) + far[part(k)].astype(F32)).astype(BF16)
        down.append(
            remote(
                ext.at[core, part(k)], ext.at[core, part(k, rows)], s4.at[k], r4.at[k],
                "tile", tile - 1,
            )
        )
        pl.when(tile > 0)(down[k].start)
        third.append(
            remote(
                ext.at[core, part(k)], ext.at[core, part(k)], s3.at[k], r3.at[k], "slab", mate
            )
        )
        third[k].start()

    @pl.when(tile < tiles - 1)
    def _():
        fifth = []
        for k in range(row_chunks):
            down[k].wait_recv()
            fifth.append(
                remote(
                    ext.at[core, part(k, rows)], ext.at[core, part(k, rows)],
                    s5.at[k], r5.at[k], "slab", mate,
                )
            )
            fifth[k].start()
        for copy in fifth:
            copy.wait()

    @pl.when(tile == tiles - 1)
    def _():
        ext[:, pl.ds(rows, rows)] = jnp.zeros((2, rows, ext.shape[2]), BF16)

    for copy in third + id_copies:
        copy.wait()
    own_ids.wait()
    for copy in first + second:
        copy.wait_send()

    @pl.when(tile > 0)
    def _():
        for copy in down:
            copy.wait_send()


def project(rolled, ids, tiles, angles):
    rows, columns = rolled.shape[1:]
    vmem = pl.BlockSpec(memory_space=pltpu.VMEM)
    sems = [pltpu.SemaphoreType.DMA((row_chunks,))] * 10
    sems += [pltpu.SemaphoreType.DMA((angles,))] * 2
    return pl.pallas_call(
        functools.partial(project_kernel, tiles, angles),
        out_shape=(
            jax.ShapeDtypeStruct((2, 2 * rows, columns), BF16),
            jax.ShapeDtypeStruct((angles,) + ids.shape, jnp.int32),
        ),
        in_specs=[vmem, vmem],
        out_specs=(vmem, vmem),
        scratch_shapes=[pltpu.VMEM((rows, columns), BF16)] * 3 + sems + [pltpu.SemaphoreType.DMA],
        compiler_params=pltpu.CompilerParams(
            collective_id=0, has_side_effects=True, vmem_limit_bytes=24 * MIB
        ),
    )(rolled, ids)


def dot(left, right):
    return jnp.dot(left, right, preferred_element_type=F32)


def patch_gradient(phase, absorb, probe_real, probe_imag, pattern, table_real, table_imag):
    mag = jnp.exp(-absorb)
    trans_real = mag * jnp.cos(phase)
    trans_imag = mag * jnp.sin(phase)
    wave_real = (probe_real * trans_real - probe_imag * trans_imag).astype(BF16)
    wave_imag = (probe_real * trans_imag + probe_imag * trans_real).astype(BF16)
    left_real = (dot(table_real, wave_real) - dot(table_imag, wave_imag)).astype(BF16)
    left_imag = (dot(table_real, wave_imag) + dot(table_imag, wave_real)).astype(BF16)
    far_real = dot(left_real, table_real) - dot(left_imag, table_imag)
    far_imag = dot(left_real, table_imag) + dot(left_imag, table_real)
    keeping = 1.0 - pattern * lax.rsqrt(far_real * far_real + far_imag * far_imag + floor_square)
    resid_real = (far_real * keeping).astype(BF16)
    resid_imag = (far_imag * keeping).astype(BF16)
    back_real = (dot(table_real, resid_real) + dot(table_imag, resid_imag)).astype(BF16)
    back_imag = (dot(table_real, resid_imag) - dot(table_imag, resid_real)).astype(BF16)
    exit_real = dot(back_real, table_real) + dot(back_imag, table_imag)
    exit_imag = dot(back_imag, table_real) - dot(back_real, table_imag)
    mixed_real = probe_real * exit_real + probe_imag * exit_imag
    mixed_imag = probe_real * exit_imag - probe_imag * exit_real
    final_real = trans_real * mixed_real + trans_imag * mixed_imag
    final_imag = trans_real * mixed_imag - trans_imag * mixed_real
    return final_imag, -final_real


def slots_kernel(offsets, starts, counts, ext, probe, patterns, tr, ti, out, total):
    width = patterns.shape[-1]
    tall, wide = width + 16, width + 128
    rows, columns = ext.shape[1:]
    total[...] = jnp.zeros_like(total)

    def visit(slot, carry):
        r, q = offsets[slot], starts[slot]
        r0 = pl.multiple_of(jnp.minimum((r // 16) * 16, rows - tall), 16)
        q0 = pl.multiple_of(jnp.minimum((q // 128) * 128, columns - wide), 128)
        dr, dq = r - r0, q - q0
        block = (pl.ds(r0, tall), pl.ds(q0, wide))

        def window(index):
            raw = ext[(index,) + block].astype(F32)
            raw = pltpu.roll(raw, lax.rem(wide - dq, wide), 1)[:, :width]
            return pltpu.roll(raw, lax.rem(tall - dr, tall), 0)[:width]

        grads = patch_gradient(
            window(0), window(1), probe[0], probe[1], patterns[slot].astype(F32), tr[...], ti[...]
        )
        for index in range(2):
            padded = jnp.concatenate([grads[index], jnp.zeros((16, width), F32)], axis=0)
            padded = pltpu.roll(padded, dr, 0)
            padded = jnp.concatenate([padded, jnp.zeros((tall, 128), F32)], axis=1)
            total[(index,) + block] += pltpu.roll(padded, dq, 1)
        return carry

    lax.fori_loop(0, counts[0], visit, 0)
    out[...] = total[...].astype(BF16)


def slots(offsets, starts, counts, ext, probe, patterns, tables):
    smem = pl.BlockSpec(memory_space=pltpu.SMEM)
    vmem = pl.BlockSpec(memory_space=pltpu.VMEM)
    return pl.pallas_call(
        slots_kernel,
        out_shape=jax.ShapeDtypeStruct(ext.shape, BF16),
        in_specs=[smem] * 3 + [vmem] * 5,
        out_specs=vmem,
        scratch_shapes=[pltpu.VMEM(ext.shape, F32)],
        compiler_params=pltpu.CompilerParams(vmem_limit_bytes=32 * MIB),
    )(offsets, starts, counts, ext, probe, patterns, *tables)


def reduce_kernel(
    tiles, angles, buf, planes,
    near, mine, far, spill, above,
    s1, r1, s2, r2, s3, r3, right_sem, left_sem, line_sem, sx, rx, sp, rp, sf, rf,
):
    rows = buf.shape[1] // 2
    part = rows // 2
    core, side, mate, other = slab_partners()
    tile = lax.axis_index("tile")
    angle = lax.axis_index("angle")

    barrier = pltpu.get_barrier_semaphore()
    pl.semaphore_signal(barrier, inc=1, device_id={"slab": mate}, device_id_type=MESH)
    pl.semaphore_signal(barrier, inc=1, device_id={"slab": other}, device_id_type=MESH)
    sides = [
        ("tile", tile - 1, tile > 0), ("tile", tile + 1, tile < tiles - 1),
        ("angle", angle - 1, angle > 0), ("angle", angle + 1, angle < angles - 1),
    ]
    for axis, index, here in sides:
        greet(barrier, axis, index, here)
    pl.semaphore_wait(barrier, 2 + sum(here.astype(jnp.int32) for _, _, here in sides))

    def block(below, half):
        return pl.ds(pl.multiple_of(below * rows + half * part, 16), part)

    blocks = [block(1, 1 - side), block(0, 1 - side), block(1, side), block(0, side)]
    first = [
        remote(buf.at[1 - core, rng], near.at[i], s1.at[i], r1.at[i], "slab", mate)
        for i, rng in enumerate(blocks)
    ]
    for copy in first:
        copy.start()
    second = []
    for i in range(2):
        first[i].wait_recv()
        mine[i] = (buf[core, blocks[i]].astype(F32) + near[i].astype(F32)).astype(BF16)
        second.append(remote(mine.at[i], far.at[i], s2.at[i], r2.at[i], "slab", other))
        second[i].start()

    first[2].wait_recv()
    second[0].wait_recv()
    spill[...] = (
        buf[core, blocks[2]].astype(F32) + near[2].astype(F32) + far[0].astype(F32)
    ).astype(BF16)
    down = remote(spill, above, s3, r3, "tile", tile + 1)
    pl.when(tile < tiles - 1)(down.start)

    @pl.when(tile == 0)
    def _():
        above[...] = jnp.zeros_like(above)

    first[3].wait_recv()
    second[1].wait_recv()
    pl.when(tile > 0)(down.wait_recv)
    planes[angle, core, block(0, side)] = (
        buf[core, blocks[3]].astype(F32) + near[3].astype(F32)
        + far[1].astype(F32) + above[...].astype(F32)
    ).astype(BF16)

    def quarter(origin, half):
        return planes.at[origin, core, block(0, half)]

    def to_right(origin):
        ref = quarter(origin, side)
        return remote(ref, ref, right_sem.at[origin], line_sem.at[origin], "angle", angle + 1)

    def to_left(origin):
        ref = quarter(origin, side)
        return remote(ref, ref, left_sem.at[origin], line_sem.at[origin], "angle", angle - 1)

    def to_other(origin):
        ref = quarter(origin, side)
        return remote(ref, ref, sx.at[origin], rx.at[origin], "slab", other)

    def to_mate(origin):
        ref = quarter(origin, side)
        return remote(ref, ref, sp.at[origin], rp.at[origin], "slab", mate)

    def pass_mate(origin):
        ref = quarter(origin, 1 - side)
        return remote(ref, ref, sf.at[origin], rf.at[origin], "slab", mate)

    def forward(origin):
        to_other(origin).start()
        to_mate(origin).start()

    pl.when(angle < angles - 1)(lambda: to_right(angle).start())
    pl.when(angle > 0)(lambda: to_left(angle).start())
    forward(angle)

    def share(origin):
        to_other(origin).wait_recv()
        pass_mate(origin).start()

    def step_origins(step):
        return [
            (angle - step, angle >= step),
            (angle + step, angle + step <= angles - 1),
        ]

    for step in range(1, angles + 1):
        if step < angles:
            left, right = step_origins(step)

            @pl.when(left[1])
            def _():
                to_right(left[0]).wait_recv()
                pl.when(angle < angles - 1)(lambda: to_right(left[0]).start())
                forward(left[0])

            @pl.when(right[1])
            def _():
                to_left(right[0]).wait_recv()
                pl.when(angle > 0)(lambda: to_left(right[0]).start())
                forward(right[0])

        if step == 1:
            share(angle)
        else:
            for origin, here in step_origins(step - 1):
                pl.when(here)(lambda origin=origin: share(origin))

    for origin in range(angles):
        to_other(origin).wait_send()
        to_mate(origin).wait()
        pass_mate(origin).wait()

        @pl.when((angle < angles - 1) & (origin <= angle))
        def _():
            to_right(origin).wait_send()

        @pl.when((angle > 0) & (origin >= angle))
        def _():
            to_left(origin).wait_send()

    for copy in first + second:
        copy.wait_send()
    pl.when(tile < tiles - 1)(down.wait_send)


def reduce_planes(buf, tiles, angles):
    rows, columns = buf.shape[1] // 2, buf.shape[2]
    part = rows // 2
    vmem = pl.BlockSpec(memory_space=pltpu.VMEM)
    dma = pltpu.SemaphoreType.DMA
    return pl.pallas_call(
        functools.partial(reduce_kernel, tiles, angles),
        out_shape=jax.ShapeDtypeStruct((angles, 2, rows, columns), BF16),
        in_specs=[vmem],
        out_specs=vmem,
        scratch_shapes=[
            pltpu.VMEM((4, part, columns), BF16),
            pltpu.VMEM((2, part, columns), BF16),
            pltpu.VMEM((2, part, columns), BF16),
            pltpu.VMEM((part, columns), BF16),
            pltpu.VMEM((part, columns), BF16),
            dma((4,)), dma((4,)), dma((2,)), dma((2,)), dma, dma,
        ] + [dma((angles,))] * 9,
        compiler_params=pltpu.CompilerParams(
            collective_id=1, has_side_effects=True, vmem_limit_bytes=48 * MIB
        ),
    )(buf)


def update_kernel(depth, ids, volume, planes, out):
    angles, _, _, columns = planes.shape
    layer = lax.axis_index("slab")
    total = jnp.zeros(planes.shape[2:], F32)
    for a in range(angles):
        shift = wrapped_shift(ids[a, 0, 0], layer, depth, columns)
        total += pltpu.roll(planes[a, 0].astype(F32), shift, 1)
    out[0, 0] = volume[0, 0].astype(F32) - step_size * total


def update(ids, volume, planes, depth):
    angles, _, rows, columns = planes.shape
    size = rows // 4
    return pl.pallas_call(
        functools.partial(update_kernel, depth),
        out_shape=jax.ShapeDtypeStruct(volume.shape, F32),
        grid=(2, 4),
        in_specs=[
            pl.BlockSpec(memory_space=pltpu.SMEM),
            pl.BlockSpec((1, 1, size, columns), lambda p, i: (p, 0, i, 0)),
            pl.BlockSpec((angles, 1, size, columns), lambda p, i: (0, p, i, 0)),
        ],
        out_specs=pl.BlockSpec((1, 1, size, columns), lambda p, i: (p, 0, i, 0)),
        compiler_params=pltpu.CompilerParams(vmem_limit_bytes=32 * MIB),
    )(ids, volume, planes)


def per_device(tiles, angles, slabs, volume, probe, amplitudes, offsets, starts, counts, angle_ids):
    columns = volume.shape[3]
    width = amplitudes.shape[-1]
    capacity = offsets.shape[3]
    depth = slabs * volume.shape[1]
    shift = wrapped_shift(angle_ids[0], lax.axis_index("slab"), depth, columns)
    rolled = jnp.roll(volume[:, 0], -shift, axis=-1)
    ids = jnp.broadcast_to(angle_ids[0], (8, 128))
    ext, all_ids = project(rolled, ids, tiles, angles)
    buf = slots(
        offsets.reshape(capacity), starts.reshape(capacity), counts.reshape(1), ext, probe,
        amplitudes.reshape(capacity, width, width), dft_tables(width),
    )
    planes = reduce_planes(buf, tiles, angles)
    return update(all_ids, volume, planes, depth)


def solution(mesh):
    in_specs = (
        P(None, "slab", "tile", None),
        P(),
        P("angle", "tile", "slab", None, None, None),
        P("angle", "tile", "slab", None),
        P("angle", "tile", "slab", None),
        P("angle", "tile", "slab"),
        P("angle"),
    )
    body = functools.partial(
        per_device, mesh.shape["tile"], mesh.shape["angle"], mesh.shape["slab"]
    )
    return jax.shard_map(
        body, mesh=mesh, in_specs=in_specs, out_specs=P(None, "slab", "tile", None),
        check_vma=False,
    )
```

```python
import functools

import jax
import jax.numpy as jnp
import numpy as np
from jax import lax
from jax.experimental import pallas as pl
from jax.experimental.pallas import tpu as pltpu
from jax.sharding import PartitionSpec as P

MESH = pl.DeviceIdType.MESH
BF16 = jnp.bfloat16
F32 = jnp.float32
MIB = 1024 * 1024

angle_center = 600
shear_divisor = 64
step_size = 0.03
floor_square = 0.25
project_rows = 32
reduce_rows = 32


def dft_tables(width):
    line = np.arange(width)
    phase = ((line[:, None] * line[None, :]) % width) * (2.0 * np.pi / width)
    scale = width ** (-0.5)
    return (
        jnp.asarray((np.cos(phase) * scale).astype(np.float32), BF16),
        jnp.asarray((-np.sin(phase) * scale).astype(np.float32), BF16),
    )


def wrapped_shift(angle_value, layer, depth, columns):
    sheared = jnp.right_shift((angle_value - angle_center) * (layer - depth // 2), 6)
    rest = lax.rem(sheared, jnp.int32(columns))
    return jnp.where(rest < 0, rest + columns, rest)


def remote(src, dst, send, recv, axis, index):
    return pltpu.make_async_remote_copy(
        src_ref=src, dst_ref=dst, send_sem=send, recv_sem=recv,
        device_id={axis: index}, device_id_type=MESH,
    )


def slab_partners():
    slab = lax.axis_index("slab")
    core = slab % 2
    side = slab // 2
    return core, side, slab + 1 - 2 * core, slab + 2 - 4 * side


def greet_all(barrier, sides):
    peers = jnp.int32(0)
    for axis, index, here in sides:
        if here is None:
            greet(barrier, axis, index)
            peers += 1
        else:
            pl.when(here)(functools.partial(greet, barrier, axis, index))
            peers += here.astype(jnp.int32)
    pl.semaphore_wait(barrier, peers)


def greet(barrier, axis, index):
    pl.semaphore_signal(barrier, inc=1, device_id={axis: index}, device_id_type=MESH)


def project_kernel(
    tiles, depth, ids, volume, ext,
    send, near, half, far, s1, r1, s2, r2, s3, r3, s4, r4, s5, r5,
):
    rows, columns = volume.shape[2:]
    chunks = rows // project_rows
    core, side, mate, other = slab_partners()
    tile = lax.axis_index("tile")
    shift = wrapped_shift(ids[0], lax.axis_index("slab"), depth, columns)
    back = lax.rem(columns - shift, jnp.int32(columns))

    barrier = pltpu.get_barrier_semaphore()
    sides = [
        ("slab", mate, None), ("slab", other, None),
        ("tile", tile - 1, tile > 0), ("tile", tile + 1, tile < tiles - 1),
    ]
    greet_all(barrier, sides)

    def part(k, base=0):
        return pl.ds(base + k * project_rows, project_rows)

    def rolled(index, k):
        return pltpu.roll(volume[index, 0, part(k)].astype(F32), back, 1)

    first, second, third, down = [], [], [], []
    for k in range(chunks):
        send[part(k)] = rolled(1 - core, k).astype(BF16)
        first.append(
            remote(send.at[part(k)], near.at[part(k)], s1.at[k], r1.at[k], "slab", mate)
        )
        first[k].start()
    for k in range(chunks):
        own = rolled(core, k)
        first[k].wait_recv()
        half[part(k)] = (own + near[part(k)].astype(F32)).astype(BF16)
        second.append(remote(half.at[part(k)], far.at[part(k)], s2.at[k], r2.at[k], "slab", other))
        second[k].start()

    for k in range(chunks):
        second[k].wait_recv()
        ext[core, part(k)] = (half[part(k)].astype(F32) + far[part(k)].astype(F32)).astype(BF16)
        down.append(
            remote(
                ext.at[core, part(k)], ext.at[core, part(k, rows)], s4.at[k], r4.at[k],
                "tile", tile - 1,
            )
        )
        pl.when(tile > 0)(down[k].start)
        third.append(
            remote(
                ext.at[core, part(k)], ext.at[core, part(k)], s3.at[k], r3.at[k], "slab", mate
            )
        )
        third[k].start()

    @pl.when(tile < tiles - 1)
    def _():
        fifth = []
        for k in range(chunks):
            down[k].wait_recv()
            fifth.append(
                remote(
                    ext.at[core, part(k, rows)], ext.at[core, part(k, rows)],
                    s5.at[k], r5.at[k], "slab", mate,
                )
            )
            fifth[k].start()
        for copy in fifth:
            copy.wait()

    @pl.when(tile == tiles - 1)
    def _():
        ext[:, pl.ds(rows, rows)] = jnp.zeros((2, rows, columns), BF16)

    for copy in third:
        copy.wait()
    for copy in first + second:
        copy.wait_send()

    @pl.when(tile > 0)
    def _():
        for copy in down:
            copy.wait_send()


def project(ids, volume, tiles, depth):
    rows, columns = volume.shape[2:]
    vmem = pl.BlockSpec(memory_space=pltpu.VMEM)
    chunks = rows // project_rows
    return pl.pallas_call(
        functools.partial(project_kernel, tiles, depth),
        out_shape=jax.ShapeDtypeStruct((2, 2 * rows, columns), BF16),
        in_specs=[pl.BlockSpec(memory_space=pltpu.SMEM), vmem],
        out_specs=vmem,
        scratch_shapes=[pltpu.VMEM((rows, columns), BF16)] * 4
        + [pltpu.SemaphoreType.DMA((chunks,))] * 10,
        compiler_params=pltpu.CompilerParams(
            collective_id=0, has_side_effects=True, vmem_limit_bytes=24 * MIB
        ),
    )(ids, volume)


def dot(left, right):
    return jnp.dot(left, right, preferred_element_type=F32)


def patch_gradient(phase, absorb, probe_real, probe_imag, pattern, table_real, table_imag):
    mag = jnp.exp(-absorb)
    trans_real = mag * jnp.cos(phase)
    trans_imag = mag * jnp.sin(phase)
    wave_real = (probe_real * trans_real - probe_imag * trans_imag).astype(BF16)
    wave_imag = (probe_real * trans_imag + probe_imag * trans_real).astype(BF16)
    left_real = (dot(table_real, wave_real) - dot(table_imag, wave_imag)).astype(BF16)
    left_imag = (dot(table_real, wave_imag) + dot(table_imag, wave_real)).astype(BF16)
    far_real = dot(left_real, table_real) - dot(left_imag, table_imag)
    far_imag = dot(left_real, table_imag) + dot(left_imag, table_real)
    keeping = 1.0 - pattern * lax.rsqrt(far_real * far_real + far_imag * far_imag + floor_square)
    resid_real = (far_real * keeping).astype(BF16)
    resid_imag = (far_imag * keeping).astype(BF16)
    back_real = (dot(table_real, resid_real) + dot(table_imag, resid_imag)).astype(BF16)
    back_imag = (dot(table_real, resid_imag) - dot(table_imag, resid_real)).astype(BF16)
    exit_real = dot(back_real, table_real) + dot(back_imag, table_imag)
    exit_imag = dot(back_imag, table_real) - dot(back_real, table_imag)
    mixed_real = probe_real * exit_real + probe_imag * exit_imag
    mixed_imag = probe_real * exit_imag - probe_imag * exit_real
    final_real = trans_real * mixed_real + trans_imag * mixed_imag
    final_imag = trans_real * mixed_imag - trans_imag * mixed_real
    return final_imag, -final_real


def slots_kernel(offsets, starts, counts, ext, probe, patterns, tr, ti, out, total):
    width = patterns.shape[-1]
    tall, wide = width + 16, width + 128
    rows, columns = ext.shape[1:]
    total[...] = jnp.zeros_like(total)

    def visit(slot, carry):
        r, q = offsets[slot], starts[slot]
        r0 = pl.multiple_of(jnp.minimum((r // 16) * 16, rows - tall), 16)
        q0 = pl.multiple_of(jnp.minimum((q // 128) * 128, columns - wide), 128)
        dr, dq = r - r0, q - q0
        block = (pl.ds(r0, tall), pl.ds(q0, wide))

        def window(index):
            raw = ext[(index,) + block].astype(F32)
            raw = pltpu.roll(raw, lax.rem(wide - dq, wide), 1)[:, :width]
            return pltpu.roll(raw, lax.rem(tall - dr, tall), 0)[:width]

        grads = patch_gradient(
            window(0), window(1), probe[0], probe[1], patterns[slot].astype(F32), tr[...], ti[...]
        )
        for index in range(2):
            padded = jnp.concatenate([grads[index], jnp.zeros((16, width), F32)], axis=0)
            padded = pltpu.roll(padded, dr, 0)
            padded = jnp.concatenate([padded, jnp.zeros((tall, 128), F32)], axis=1)
            total[(index,) + block] += pltpu.roll(padded, dq, 1)
        return carry

    lax.fori_loop(0, counts[0], visit, 0)
    out[...] = total[...].astype(BF16)


def slots(offsets, starts, counts, ext, probe, patterns, tables):
    smem = pl.BlockSpec(memory_space=pltpu.SMEM)
    vmem = pl.BlockSpec(memory_space=pltpu.VMEM)
    return pl.pallas_call(
        slots_kernel,
        out_shape=jax.ShapeDtypeStruct(ext.shape, BF16),
        in_specs=[smem] * 3 + [vmem] * 5,
        out_specs=vmem,
        scratch_shapes=[pltpu.VMEM(ext.shape, F32)],
        compiler_params=pltpu.CompilerParams(vmem_limit_bytes=32 * MIB),
    )(offsets, starts, counts, ext, probe, patterns, *tables)


def reduce_kernel(
    tiles, angles, depth, ids, volume, buf, out,
    near, near_below, below, above, mine, far, plane, own,
    from_left, from_right, send_right, send_left,
    s1, r1, s2, r2, s3, r3, s4, r4, s5, r5, s6, r6, s7, r7,
):
    rows, columns = volume.shape[2:]
    size = reduce_rows
    chunks = rows // size
    core, side, mate, other = slab_partners()
    tile = lax.axis_index("tile")
    angle = lax.axis_index("angle")
    shift = wrapped_shift(ids[0], lax.axis_index("slab"), depth, columns)
    has_next, has_previous = tile < tiles - 1, tile > 0
    has_right, has_left = angle < angles - 1, angle > 0
    left_is_near = angle < angles // 2

    greet_all(pltpu.get_barrier_semaphore(), [
        ("slab", mate, None), ("slab", other, None),
        ("tile", tile - 1, has_previous), ("tile", tile + 1, has_next),
        ("angle", angle - 1, has_left), ("angle", angle + 1, has_right),
    ])

    def part(k, base=0):
        return pl.ds(base + k * size, size)

    def wide(ref, k):
        return ref[:, part(k)].astype(F32)

    def below_copy(k):
        return remote(
            buf.at[1 - core, part(k, rows)], near_below.at[part(k)], s1.at[k], r1.at[k],
            "slab", mate,
        )

    def near_copy(k):
        return remote(
            buf.at[1 - core, part(k)], near.at[part(k)], s2.at[k], r2.at[k], "slab", mate
        )

    def down_copy(k):
        return remote(below.at[part(k)], above.at[part(k)], s3.at[k], r3.at[k], "tile", tile + 1)

    def far_copy(k):
        return remote(mine.at[part(k)], far.at[part(k)], s4.at[k], r4.at[k], "slab", other)

    def plane_copy(k):
        ref = plane.at[core, part(k)]
        return remote(ref, ref, s5.at[k], r5.at[k], "slab", mate)

    def right_copy(k):
        return remote(
            send_right.at[:, part(k)], from_left.at[:, part(k)], s6.at[k], r6.at[k],
            "angle", angle + 1,
        )

    def left_copy(k):
        return remote(
            send_left.at[:, part(k)], from_right.at[:, part(k)], s7.at[k], r7.at[k],
            "angle", angle - 1,
        )

    for k in range(chunks):
        pl.when(has_next)(lambda k=k: below_copy(k).start())
        near_copy(k).start()

    @pl.when(jnp.logical_not(has_previous))
    def _():
        above[...] = jnp.zeros_like(above)

    @pl.when(jnp.logical_not(has_left))
    def _():
        from_left[...] = jnp.zeros_like(from_left)

    @pl.when(jnp.logical_not(has_right))
    def _():
        from_right[...] = jnp.zeros_like(from_right)

    def pass_below(k):
        below_copy(k).wait_recv()
        below[part(k)] = (
            buf[core, part(k, rows)].astype(F32) + near_below[part(k)].astype(F32)
        ).astype(BF16)
        down_copy(k).start()

    def pair_sum(k):
        near_copy(k).wait_recv()
        pl.when(has_previous)(lambda: down_copy(k).wait_recv())
        mine[part(k)] = (
            buf[core, part(k)].astype(F32)
            + near[part(k)].astype(F32)
            + above[part(k)].astype(F32)
        ).astype(BF16)
        far_copy(k).start()

    def slab_sum(k):
        far_copy(k).wait_recv()
        plane[core, part(k)] = (
            mine[part(k)].astype(F32) + far[part(k)].astype(F32)
        ).astype(BF16)
        plane_copy(k).start()

    def roll_own(k):
        plane_copy(k).wait_recv()
        for index in range(2):
            own[index, part(k)] = pltpu.roll(plane[index, part(k)].astype(F32), shift, 1)

        @pl.when(jnp.logical_not(has_left) & has_right)
        def _():
            send_right[:, part(k)] = own[:, part(k)].astype(BF16)
            right_copy(k).start()

        @pl.when(jnp.logical_not(has_right) & has_left)
        def _():
            send_left[:, part(k)] = own[:, part(k)].astype(BF16)
            left_copy(k).start()

    def move_right(k):
        right_copy(k).wait_recv()

        @pl.when(has_right)
        def _():
            send_right[:, part(k)] = (own[:, part(k)] + wide(from_left, k)).astype(BF16)
            right_copy(k).start()

    def move_left(k):
        left_copy(k).wait_recv()

        @pl.when(has_left)
        def _():
            send_left[:, part(k)] = (own[:, part(k)] + wide(from_right, k)).astype(BF16)
            left_copy(k).start()

    def near_angles(k):
        pl.when(left_is_near & has_left)(lambda: move_right(k))
        pl.when(jnp.logical_not(left_is_near) & has_right)(lambda: move_left(k))

    def far_angles(k):
        pl.when(left_is_near & has_right)(lambda: move_left(k))
        pl.when(jnp.logical_not(left_is_near) & has_left)(lambda: move_right(k))
        total = own[:, part(k)] + wide(from_left, k) + wide(from_right, k)
        out[:, 0, part(k)] = volume[:, 0, part(k)].astype(F32) - step_size * total

    stages = [
        (0, lambda k: pl.when(has_next)(lambda: pass_below(k))),
        (0, pair_sum), (1, slab_sum), (2, roll_own), (3, near_angles), (5, far_angles),
    ]
    for tick in range(chunks + 5):
        for lag, stage in stages:
            if 0 <= tick - lag < chunks:
                stage(tick - lag)

    for k in range(chunks):
        near_copy(k).wait_send()
        far_copy(k).wait_send()
        plane_copy(k).wait_send()

        @pl.when(has_next)
        def _():
            below_copy(k).wait_send()
            down_copy(k).wait_send()

        pl.when(has_right)(lambda: right_copy(k).wait_send())
        pl.when(has_left)(lambda: left_copy(k).wait_send())


def reduce_update(ids, volume, buf, tiles, angles, depth):
    rows, columns = volume.shape[2:]
    vmem = pl.BlockSpec(memory_space=pltpu.VMEM)
    single = pltpu.VMEM((rows, columns), BF16)
    double = pltpu.VMEM((2, rows, columns), BF16)
    return pl.pallas_call(
        functools.partial(reduce_kernel, tiles, angles, depth),
        out_shape=jax.ShapeDtypeStruct(volume.shape, F32),
        in_specs=[pl.BlockSpec(memory_space=pltpu.SMEM), vmem, vmem],
        out_specs=vmem,
        scratch_shapes=[single] * 6
        + [double, pltpu.VMEM((2, rows, columns), F32)]
        + [double] * 4
        + [pltpu.SemaphoreType.DMA((rows // reduce_rows,))] * 14,
        compiler_params=pltpu.CompilerParams(
            collective_id=1, has_side_effects=True, vmem_limit_bytes=40 * MIB
        ),
    )(ids, volume, buf)


def per_device(tiles, angles, slabs, volume, probe, amplitudes, offsets, starts, counts, angle_ids):
    width = amplitudes.shape[-1]
    capacity = offsets.shape[3]
    depth = slabs * volume.shape[1]
    ext = project(angle_ids, volume, tiles, depth)
    buf = slots(
        offsets.reshape(capacity), starts.reshape(capacity), counts.reshape(1), ext, probe,
        amplitudes.reshape(capacity, width, width), dft_tables(width),
    )
    return reduce_update(angle_ids, volume, buf, tiles, angles, depth)


def solution(mesh):
    in_specs = (
        P(None, "slab", "tile", None),
        P(),
        P("angle", "tile", "slab", None, None, None),
        P("angle", "tile", "slab", None),
        P("angle", "tile", "slab", None),
        P("angle", "tile", "slab"),
        P("angle"),
    )
    body = functools.partial(
        per_device, mesh.shape["tile"], mesh.shape["angle"], mesh.shape["slab"]
    )
    return jax.shard_map(
        body, mesh=mesh, in_specs=in_specs, out_specs=P(None, "slab", "tile", None),
        check_vma=False,
    )
```

```python
import functools

import jax
import jax.numpy as jnp
import numpy as np
from jax import lax
from jax.experimental import pallas as pl
from jax.experimental.pallas import tpu as pltpu
from jax.sharding import PartitionSpec as P

MESH = pl.DeviceIdType.MESH
BF16 = jnp.bfloat16
F32 = jnp.float32
MIB = 1024 * 1024

angle_center = 600
shear_divisor = 64
step_size = 0.03
floor_square = 0.25
project_rows = 16
reduce_rows = 16


def dft_tables(width):
    line = np.arange(width)
    phase = ((line[:, None] * line[None, :]) % width) * (2.0 * np.pi / width)
    scale = width ** (-0.5)
    return (
        jnp.asarray((np.cos(phase) * scale).astype(np.float32), BF16),
        jnp.asarray((-np.sin(phase) * scale).astype(np.float32), BF16),
    )


def wrapped_shift(angle_value, layer, depth, columns):
    sheared = jnp.right_shift((angle_value - angle_center) * (layer - depth // 2), 6)
    rest = lax.rem(sheared, jnp.int32(columns))
    return jnp.where(rest < 0, rest + columns, rest)


def remote(src, dst, send, recv, axis, index):
    return pltpu.make_async_remote_copy(
        src_ref=src, dst_ref=dst, send_sem=send, recv_sem=recv,
        device_id={axis: index}, device_id_type=MESH,
    )


def slab_partners():
    slab = lax.axis_index("slab")
    core = slab % 2
    side = slab // 2
    return core, side, slab + 1 - 2 * core, slab + 2 - 4 * side


def greet_all(barrier, sides):
    peers = jnp.int32(0)
    for axis, index, here in sides:
        if here is None:
            greet(barrier, axis, index)
            peers += 1
        else:
            pl.when(here)(functools.partial(greet, barrier, axis, index))
            peers += here.astype(jnp.int32)
    pl.semaphore_wait(barrier, peers)


def greet(barrier, axis, index):
    pl.semaphore_signal(barrier, inc=1, device_id={axis: index}, device_id_type=MESH)


def project_kernel(
    tiles, depth, ids, volume, ext,
    send, near, half, far, s1, r1, s2, r2, s3, r3, s4, r4, s5, r5,
):
    rows, columns = volume.shape[2:]
    chunks = rows // project_rows
    core, side, mate, other = slab_partners()
    tile = lax.axis_index("tile")
    shift = wrapped_shift(ids[0], lax.axis_index("slab"), depth, columns)
    back = lax.rem(columns - shift, jnp.int32(columns))

    barrier = pltpu.get_barrier_semaphore()
    sides = [
        ("slab", mate, None), ("slab", other, None),
        ("tile", tile - 1, tile > 0), ("tile", tile + 1, tile < tiles - 1),
    ]
    greet_all(barrier, sides)

    def part(k, base=0):
        return pl.ds(base + k * project_rows, project_rows)

    def rolled(index, k):
        return pltpu.roll(volume[index, 0, part(k)].astype(F32), back, 1)

    first, second, third, down = [], [], [], []
    for k in range(chunks):
        send[part(k)] = rolled(1 - core, k).astype(BF16)
        first.append(
            remote(send.at[part(k)], near.at[part(k)], s1.at[k], r1.at[k], "slab", mate)
        )
        first[k].start()
    for k in range(chunks):
        own = rolled(core, k)
        first[k].wait_recv()
        half[part(k)] = (own + near[part(k)].astype(F32)).astype(BF16)
        second.append(remote(half.at[part(k)], far.at[part(k)], s2.at[k], r2.at[k], "slab", other))
        second[k].start()

    for k in range(chunks):
        second[k].wait_recv()
        ext[core, part(k)] = (half[part(k)].astype(F32) + far[part(k)].astype(F32)).astype(BF16)
        down.append(
            remote(
                ext.at[core, part(k)], ext.at[core, part(k, rows)], s4.at[k], r4.at[k],
                "tile", tile - 1,
            )
        )
        pl.when(tile > 0)(down[k].start)
        third.append(
            remote(
                ext.at[core, part(k)], ext.at[core, part(k)], s3.at[k], r3.at[k], "slab", mate
            )
        )
        third[k].start()

    @pl.when(tile < tiles - 1)
    def _():
        fifth = []
        for k in range(chunks):
            down[k].wait_recv()
            fifth.append(
                remote(
                    ext.at[core, part(k, rows)], ext.at[core, part(k, rows)],
                    s5.at[k], r5.at[k], "slab", mate,
                )
            )
            fifth[k].start()
        for copy in fifth:
            copy.wait()

    @pl.when(tile == tiles - 1)
    def _():
        ext[:, pl.ds(rows, rows)] = jnp.zeros((2, rows, columns), BF16)

    for copy in third:
        copy.wait()
    for copy in first + second:
        copy.wait_send()

    @pl.when(tile > 0)
    def _():
        for copy in down:
            copy.wait_send()


def project(ids, volume, tiles, depth):
    rows, columns = volume.shape[2:]
    vmem = pl.BlockSpec(memory_space=pltpu.VMEM)
    chunks = rows // project_rows
    return pl.pallas_call(
        functools.partial(project_kernel, tiles, depth),
        out_shape=jax.ShapeDtypeStruct((2, 2 * rows, columns), BF16),
        in_specs=[pl.BlockSpec(memory_space=pltpu.SMEM), vmem],
        out_specs=vmem,
        scratch_shapes=[pltpu.VMEM((rows, columns), BF16)] * 4
        + [pltpu.SemaphoreType.DMA((chunks,))] * 10,
        compiler_params=pltpu.CompilerParams(
            collective_id=0, has_side_effects=True, vmem_limit_bytes=24 * MIB
        ),
    )(ids, volume)


def dot(left, right):
    return jnp.dot(left, right, preferred_element_type=F32)


def patch_gradient(phase, absorb, probe_real, probe_imag, pattern, table_real, table_imag):
    mag = jnp.exp(-absorb)
    trans_real = mag * jnp.cos(phase)
    trans_imag = mag * jnp.sin(phase)
    wave_real = (probe_real * trans_real - probe_imag * trans_imag).astype(BF16)
    wave_imag = (probe_real * trans_imag + probe_imag * trans_real).astype(BF16)
    left_real = (dot(table_real, wave_real) - dot(table_imag, wave_imag)).astype(BF16)
    left_imag = (dot(table_real, wave_imag) + dot(table_imag, wave_real)).astype(BF16)
    far_real = dot(left_real, table_real) - dot(left_imag, table_imag)
    far_imag = dot(left_real, table_imag) + dot(left_imag, table_real)
    keeping = 1.0 - pattern * lax.rsqrt(far_real * far_real + far_imag * far_imag + floor_square)
    resid_real = (far_real * keeping).astype(BF16)
    resid_imag = (far_imag * keeping).astype(BF16)
    back_real = (dot(table_real, resid_real) + dot(table_imag, resid_imag)).astype(BF16)
    back_imag = (dot(table_real, resid_imag) - dot(table_imag, resid_real)).astype(BF16)
    exit_real = dot(back_real, table_real) + dot(back_imag, table_imag)
    exit_imag = dot(back_imag, table_real) - dot(back_real, table_imag)
    mixed_real = probe_real * exit_real + probe_imag * exit_imag
    mixed_imag = probe_real * exit_imag - probe_imag * exit_real
    final_real = trans_real * mixed_real + trans_imag * mixed_imag
    final_imag = trans_real * mixed_imag - trans_imag * mixed_real
    return final_imag, -final_real


def slots_kernel(offsets, starts, counts, ext, probe, patterns, tr, ti, out, total):
    width = patterns.shape[-1]
    tall, wide = width + 16, width + 128
    rows, columns = ext.shape[1:]
    total[...] = jnp.zeros_like(total)

    def visit(slot, carry):
        r, q = offsets[slot], starts[slot]
        r0 = pl.multiple_of(jnp.minimum((r // 16) * 16, rows - tall), 16)
        q0 = pl.multiple_of(jnp.minimum((q // 128) * 128, columns - wide), 128)
        dr, dq = r - r0, q - q0
        block = (pl.ds(r0, tall), pl.ds(q0, wide))

        def window(index):
            raw = ext[(index,) + block].astype(F32)
            raw = pltpu.roll(raw, lax.rem(wide - dq, wide), 1)[:, :width]
            return pltpu.roll(raw, lax.rem(tall - dr, tall), 0)[:width]

        grads = patch_gradient(
            window(0), window(1), probe[0], probe[1], patterns[slot].astype(F32), tr[...], ti[...]
        )
        for index in range(2):
            padded = jnp.concatenate([grads[index], jnp.zeros((16, width), F32)], axis=0)
            padded = pltpu.roll(padded, dr, 0)
            padded = jnp.concatenate([padded, jnp.zeros((tall, 128), F32)], axis=1)
            total[(index,) + block] += pltpu.roll(padded, dq, 1)
        return carry

    lax.fori_loop(0, counts[0], visit, 0)
    out[...] = total[...].astype(BF16)


def slots(offsets, starts, counts, ext, probe, patterns, tables):
    smem = pl.BlockSpec(memory_space=pltpu.SMEM)
    vmem = pl.BlockSpec(memory_space=pltpu.VMEM)
    return pl.pallas_call(
        slots_kernel,
        out_shape=jax.ShapeDtypeStruct(ext.shape, BF16),
        in_specs=[smem] * 3 + [vmem] * 5,
        out_specs=vmem,
        scratch_shapes=[pltpu.VMEM(ext.shape, F32)],
        compiler_params=pltpu.CompilerParams(vmem_limit_bytes=32 * MIB),
    )(offsets, starts, counts, ext, probe, patterns, *tables)


def reduce_kernel(
    tiles, angles, depth, ids, volume, buf, out,
    near, near_below, below, above, mine, far, plane, own,
    from_left, from_right, send_right, send_left,
    s1, r1, s2, r2, s3, r3, s4, r4, s5, r5, s6, r6, s7, r7,
):
    rows, columns = volume.shape[2:]
    size = reduce_rows
    chunks = rows // size
    core, side, mate, other = slab_partners()
    tile = lax.axis_index("tile")
    angle = lax.axis_index("angle")
    shift = wrapped_shift(ids[0], lax.axis_index("slab"), depth, columns)
    has_next, has_previous = tile < tiles - 1, tile > 0
    has_right, has_left = angle < angles - 1, angle > 0
    left_is_near = angle < angles // 2
    inside = has_left & has_right

    greet_all(pltpu.get_barrier_semaphore(), [
        ("slab", mate, None), ("slab", other, None),
        ("tile", tile - 1, has_previous), ("tile", tile + 1, has_next),
        ("angle", angle - 1, has_left), ("angle", angle + 1, has_right),
    ])

    def part(k, base=0):
        return pl.ds(base + k * size, size)

    def wide(ref, k):
        return ref[:, part(k)].astype(F32)

    def below_copy(k):
        return remote(
            buf.at[1 - core, part(k, rows)], near_below.at[part(k)], s1.at[k], r1.at[k],
            "slab", mate,
        )

    def near_copy(k):
        return remote(
            buf.at[1 - core, part(k)], near.at[part(k)], s2.at[k], r2.at[k], "slab", mate
        )

    def down_copy(k):
        return remote(below.at[part(k)], above.at[part(k)], s3.at[k], r3.at[k], "tile", tile + 1)

    def far_copy(k):
        return remote(mine.at[part(k)], far.at[part(k)], s4.at[k], r4.at[k], "slab", other)

    def plane_copy(k):
        ref = plane.at[core, part(k)]
        return remote(ref, ref, s5.at[k], r5.at[k], "slab", mate)

    def right_copy(k):
        return remote(
            send_right.at[:, part(k)], from_left.at[:, part(k)], s6.at[k], r6.at[k],
            "angle", angle + 1,
        )

    def left_copy(k):
        return remote(
            send_left.at[:, part(k)], from_right.at[:, part(k)], s7.at[k], r7.at[k],
            "angle", angle - 1,
        )

    for k in range(chunks):
        pl.when(has_next)(lambda k=k: below_copy(k).start())
        near_copy(k).start()

    @pl.when(jnp.logical_not(has_previous))
    def _():
        above[...] = jnp.zeros_like(above)

    @pl.when(jnp.logical_not(has_left))
    def _():
        from_left[...] = jnp.zeros_like(from_left)

    @pl.when(jnp.logical_not(has_right))
    def _():
        from_right[...] = jnp.zeros_like(from_right)

    def pass_below(k):
        below_copy(k).wait_recv()
        below[part(k)] = (
            buf[core, part(k, rows)].astype(F32) + near_below[part(k)].astype(F32)
        ).astype(BF16)
        down_copy(k).start()

    def pair_sum(k):
        near_copy(k).wait_recv()
        pl.when(has_previous)(lambda: down_copy(k).wait_recv())
        mine[part(k)] = (
            buf[core, part(k)].astype(F32)
            + near[part(k)].astype(F32)
            + above[part(k)].astype(F32)
        ).astype(BF16)
        far_copy(k).start()

    def slab_sum(k):
        far_copy(k).wait_recv()
        plane[core, part(k)] = (
            mine[part(k)].astype(F32) + far[part(k)].astype(F32)
        ).astype(BF16)
        plane_copy(k).start()

    def roll_own(k):
        plane_copy(k).wait_recv()
        for index in range(2):
            own[index, part(k)] = pltpu.roll(plane[index, part(k)].astype(F32), shift, 1)

        @pl.when(jnp.logical_not(has_left) & has_right)
        def _():
            send_right[:, part(k)] = own[:, part(k)].astype(BF16)
            right_copy(k).start()

        @pl.when(jnp.logical_not(has_right) & has_left)
        def _():
            send_left[:, part(k)] = own[:, part(k)].astype(BF16)
            left_copy(k).start()

    def move_right(k):
        right_copy(k).wait_recv()

        @pl.when(has_right)
        def _():
            send_right[:, part(k)] = (own[:, part(k)] + wide(from_left, k)).astype(BF16)
            right_copy(k).start()

    def move_left(k):
        left_copy(k).wait_recv()

        @pl.when(has_left)
        def _():
            send_left[:, part(k)] = (own[:, part(k)] + wide(from_right, k)).astype(BF16)
            left_copy(k).start()

    def near_angles(k):
        pl.when(left_is_near & has_left)(lambda: move_right(k))
        pl.when(jnp.logical_not(left_is_near) & has_right)(lambda: move_left(k))

    def far_angles(k):
        pl.when(left_is_near & has_right)(lambda: move_left(k))
        pl.when(jnp.logical_not(left_is_near) & has_left)(lambda: move_right(k))
        total = own[:, part(k)] + wide(from_left, k) + wide(from_right, k)
        out[:, 0, part(k)] = volume[:, 0, part(k)].astype(F32) - step_size * total

    stages = [
        (0, lambda k: pl.when(has_next)(lambda: pass_below(k))),
        (0, pair_sum), (1, slab_sum), (2, roll_own), (3, near_angles),
        (5, lambda k: pl.when(inside)(lambda: far_angles(k))),
    ]
    for tick in range(chunks + 5):
        for lag, stage in stages:
            if 0 <= tick - lag < chunks:
                stage(tick - lag)

    @pl.when(jnp.logical_not(inside))
    def _():
        for k in range(chunks):
            far_angles(k)

    for k in range(chunks):
        near_copy(k).wait_send()
        far_copy(k).wait_send()
        plane_copy(k).wait_send()

        @pl.when(has_next)
        def _():
            below_copy(k).wait_send()
            down_copy(k).wait_send()

        pl.when(has_right)(lambda: right_copy(k).wait_send())
        pl.when(has_left)(lambda: left_copy(k).wait_send())


def reduce_update(ids, volume, buf, tiles, angles, depth):
    rows, columns = volume.shape[2:]
    vmem = pl.BlockSpec(memory_space=pltpu.VMEM)
    single = pltpu.VMEM((rows, columns), BF16)
    double = pltpu.VMEM((2, rows, columns), BF16)
    return pl.pallas_call(
        functools.partial(reduce_kernel, tiles, angles, depth),
        out_shape=jax.ShapeDtypeStruct(volume.shape, F32),
        in_specs=[pl.BlockSpec(memory_space=pltpu.SMEM), vmem, vmem],
        out_specs=vmem,
        scratch_shapes=[single] * 6
        + [double, pltpu.VMEM((2, rows, columns), F32)]
        + [double] * 4
        + [pltpu.SemaphoreType.DMA((rows // reduce_rows,))] * 14,
        compiler_params=pltpu.CompilerParams(
            collective_id=1, has_side_effects=True, vmem_limit_bytes=40 * MIB
        ),
    )(ids, volume, buf)


def per_device(tiles, angles, slabs, volume, probe, amplitudes, offsets, starts, counts, angle_ids):
    width = amplitudes.shape[-1]
    capacity = offsets.shape[3]
    depth = slabs * volume.shape[1]
    ext = project(angle_ids, volume, tiles, depth)
    buf = slots(
        offsets.reshape(capacity), starts.reshape(capacity), counts.reshape(1), ext, probe,
        amplitudes.reshape(capacity, width, width), dft_tables(width),
    )
    return reduce_update(angle_ids, volume, buf, tiles, angles, depth)


def solution(mesh):
    in_specs = (
        P(None, "slab", "tile", None),
        P(),
        P("angle", "tile", "slab", None, None, None),
        P("angle", "tile", "slab", None),
        P("angle", "tile", "slab", None),
        P("angle", "tile", "slab"),
        P("angle"),
    )
    body = functools.partial(
        per_device, mesh.shape["tile"], mesh.shape["angle"], mesh.shape["slab"]
    )
    return jax.shard_map(
        body, mesh=mesh, in_specs=in_specs, out_specs=P(None, "slab", "tile", None),
        check_vma=False,
    )
```

```python
import functools

import jax
import jax.numpy as jnp
import numpy as np
from jax import lax
from jax.experimental import pallas as pl
from jax.experimental.pallas import tpu as pltpu
from jax.sharding import PartitionSpec as P

MESH = pl.DeviceIdType.MESH
BF16 = jnp.bfloat16
F32 = jnp.float32
MIB = 1024 * 1024

angle_center = 600
shear_divisor = 64
step_size = 0.03
floor_square = 0.25
project_rows = 16
reduce_rows = 16


def dft_tables(width):
    line = np.arange(width)
    phase = ((line[:, None] * line[None, :]) % width) * (2.0 * np.pi / width)
    scale = width ** (-0.5)
    return (
        jnp.asarray((np.cos(phase) * scale).astype(np.float32), BF16),
        jnp.asarray((-np.sin(phase) * scale).astype(np.float32), BF16),
    )


def wrapped_shift(angle_value, layer, depth, columns):
    sheared = jnp.right_shift((angle_value - angle_center) * (layer - depth // 2), 6)
    rest = lax.rem(sheared, jnp.int32(columns))
    return jnp.where(rest < 0, rest + columns, rest)


def remote(src, dst, send, recv, axis, index):
    return pltpu.make_async_remote_copy(
        src_ref=src, dst_ref=dst, send_sem=send, recv_sem=recv,
        device_id={axis: index}, device_id_type=MESH,
    )


def slab_partners():
    slab = lax.axis_index("slab")
    core = slab % 2
    side = slab // 2
    return core, side, slab + 1 - 2 * core, slab + 2 - 4 * side


def greet_all(barrier, sides):
    peers = jnp.int32(0)
    for axis, index, here in sides:
        if here is None:
            greet(barrier, axis, index)
            peers += 1
        else:
            pl.when(here)(functools.partial(greet, barrier, axis, index))
            peers += here.astype(jnp.int32)
    pl.semaphore_wait(barrier, peers)


def greet(barrier, axis, index):
    pl.semaphore_signal(barrier, inc=1, device_id={axis: index}, device_id_type=MESH)


def project_kernel(
    tiles, depth, ids, source, ext,
    volume, send, near, half, far, s1, r1, s2, r2, s3, r3, s4, r4, s5, r5, loads,
):
    rows, columns = source.shape[2:]
    chunks = rows // project_rows
    core, side, mate, other = slab_partners()
    tile = lax.axis_index("tile")
    shift = wrapped_shift(ids[0], lax.axis_index("slab"), depth, columns)
    back = lax.rem(columns - shift, jnp.int32(columns))
    parts = (1 - core, core)
    fetched = [
        pltpu.make_async_copy(source.at[parts[i], 0], volume.at[parts[i]], loads.at[i])
        for i in range(2)
    ]
    for copy in fetched:
        copy.start()

    barrier = pltpu.get_barrier_semaphore()
    sides = [
        ("slab", mate, None), ("slab", other, None),
        ("tile", tile - 1, tile > 0), ("tile", tile + 1, tile < tiles - 1),
    ]
    greet_all(barrier, sides)

    def part(k, base=0):
        return pl.ds(base + k * project_rows, project_rows)

    def rolled(index, k):
        return pltpu.roll(volume[index, part(k)].astype(F32), back, 1)

    first, second, third, down = [], [], [], []
    fetched[0].wait()
    for k in range(chunks):
        send[part(k)] = rolled(1 - core, k).astype(BF16)
        first.append(
            remote(send.at[part(k)], near.at[part(k)], s1.at[k], r1.at[k], "slab", mate)
        )
        first[k].start()
    fetched[1].wait()
    for k in range(chunks):
        own = rolled(core, k)
        first[k].wait_recv()
        half[part(k)] = (own + near[part(k)].astype(F32)).astype(BF16)
        second.append(remote(half.at[part(k)], far.at[part(k)], s2.at[k], r2.at[k], "slab", other))
        second[k].start()

    for k in range(chunks):
        second[k].wait_recv()
        ext[core, part(k)] = (half[part(k)].astype(F32) + far[part(k)].astype(F32)).astype(BF16)
        down.append(
            remote(
                ext.at[core, part(k)], ext.at[core, part(k, rows)], s4.at[k], r4.at[k],
                "tile", tile - 1,
            )
        )
        pl.when(tile > 0)(down[k].start)
        third.append(
            remote(
                ext.at[core, part(k)], ext.at[core, part(k)], s3.at[k], r3.at[k], "slab", mate
            )
        )
        third[k].start()

    @pl.when(tile < tiles - 1)
    def _():
        fifth = []
        for k in range(chunks):
            down[k].wait_recv()
            fifth.append(
                remote(
                    ext.at[core, part(k, rows)], ext.at[core, part(k, rows)],
                    s5.at[k], r5.at[k], "slab", mate,
                )
            )
            fifth[k].start()
        for copy in fifth:
            copy.wait()

    @pl.when(tile == tiles - 1)
    def _():
        ext[:, pl.ds(rows, rows)] = jnp.zeros((2, rows, columns), BF16)

    for copy in third:
        copy.wait()
    for copy in first + second:
        copy.wait_send()

    @pl.when(tile > 0)
    def _():
        for copy in down:
            copy.wait_send()


def project(ids, volume, tiles, depth):
    rows, columns = volume.shape[2:]
    vmem = pl.BlockSpec(memory_space=pltpu.VMEM)
    chunks = rows // project_rows
    return pl.pallas_call(
        functools.partial(project_kernel, tiles, depth),
        out_shape=jax.ShapeDtypeStruct((2, 2 * rows, columns), BF16),
        in_specs=[
            pl.BlockSpec(memory_space=pltpu.SMEM), pl.BlockSpec(memory_space=pltpu.HBM)
        ],
        out_specs=vmem,
        scratch_shapes=[pltpu.VMEM((2, rows, columns), BF16)]
        + [pltpu.VMEM((rows, columns), BF16)] * 4
        + [pltpu.SemaphoreType.DMA((chunks,))] * 10
        + [pltpu.SemaphoreType.DMA((2,))],
        compiler_params=pltpu.CompilerParams(
            collective_id=0, has_side_effects=True, vmem_limit_bytes=24 * MIB
        ),
    )(ids, volume)


def dot(left, right):
    return jnp.dot(left, right, preferred_element_type=F32)


def sine_cosine(angle):
    turns = jnp.floor(angle * (2.0 / np.pi) + 0.5)
    rest = ((angle - turns * 1.5703125) - turns * 4.837512969970703e-4) - turns * 7.5497899548918e-8
    square = rest * rest
    sine = rest + rest * square * (
        -1.0 / 6 + square * (1.0 / 120 + square * (-1.0 / 5040 + square * (1.0 / 362880)))
    )
    cosine = 1.0 + square * (
        -0.5 + square * (1.0 / 24 + square * (-1.0 / 720 + square * (1.0 / 40320)))
    )
    quadrant = turns.astype(jnp.int32)
    odd = (quadrant & 1) != 0
    found_sine, found_cosine = jnp.where(odd, cosine, sine), jnp.where(odd, sine, cosine)
    return (
        jnp.where((quadrant & 2) != 0, -found_sine, found_sine),
        jnp.where(((quadrant + 1) & 2) != 0, -found_cosine, found_cosine),
    )


def patch_gradient(phase, absorb, probe_real, probe_imag, pattern, table_real, table_imag):
    mag = jnp.exp(-absorb)
    sine, cosine = sine_cosine(phase)
    trans_real = mag * cosine
    trans_imag = mag * sine
    wave_real = (probe_real * trans_real - probe_imag * trans_imag).astype(BF16)
    wave_imag = (probe_real * trans_imag + probe_imag * trans_real).astype(BF16)
    left_real = (dot(table_real, wave_real) - dot(table_imag, wave_imag)).astype(BF16)
    left_imag = (dot(table_real, wave_imag) + dot(table_imag, wave_real)).astype(BF16)
    far_real = dot(left_real, table_real) - dot(left_imag, table_imag)
    far_imag = dot(left_real, table_imag) + dot(left_imag, table_real)
    keeping = 1.0 - pattern * lax.rsqrt(far_real * far_real + far_imag * far_imag + floor_square)
    resid_real = (far_real * keeping).astype(BF16)
    resid_imag = (far_imag * keeping).astype(BF16)
    back_real = (dot(table_real, resid_real) + dot(table_imag, resid_imag)).astype(BF16)
    back_imag = (dot(table_real, resid_imag) - dot(table_imag, resid_real)).astype(BF16)
    exit_real = dot(back_real, table_real) + dot(back_imag, table_imag)
    exit_imag = dot(back_imag, table_real) - dot(back_real, table_imag)
    mixed_real = probe_real * exit_real + probe_imag * exit_imag
    mixed_imag = probe_real * exit_imag - probe_imag * exit_real
    final_real = trans_real * mixed_real + trans_imag * mixed_imag
    final_imag = trans_real * mixed_imag - trans_imag * mixed_real
    return final_imag, -final_real


def slots_kernel(offsets, starts, counts, ext, probe, patterns, tr, ti, out):
    width = patterns.shape[-1]
    tall, wide = width + 16, width + 128
    rows, columns = ext.shape[1:]
    out[...] = jnp.zeros_like(out)

    def visit(slot, carry):
        r, q = offsets[slot], starts[slot]
        r0 = pl.multiple_of(jnp.minimum((r // 16) * 16, rows - tall), 16)
        q0 = pl.multiple_of(jnp.minimum((q // 128) * 128, columns - wide), 128)
        dr, dq = r - r0, q - q0
        block = (pl.ds(r0, tall), pl.ds(q0, wide))

        def window(index):
            raw = ext[(index,) + block].astype(F32)
            raw = pltpu.roll(raw, lax.rem(wide - dq, wide), 1)[:, :width]
            return pltpu.roll(raw, lax.rem(tall - dr, tall), 0)[:width]

        grads = patch_gradient(
            window(0), window(1), probe[0], probe[1], patterns[slot].astype(F32), tr[...], ti[...]
        )
        for index in range(2):
            padded = jnp.concatenate([grads[index], jnp.zeros((16, width), F32)], axis=0)
            padded = pltpu.roll(padded, dr, 0)
            padded = jnp.concatenate([padded, jnp.zeros((tall, 128), F32)], axis=1)
            padded = pltpu.roll(padded, dq, 1) + out[(index,) + block].astype(F32)
            out[(index,) + block] = padded.astype(BF16)
        return carry

    lax.fori_loop(0, counts[0], visit, 0)


def slots(offsets, starts, counts, ext, probe, patterns, tables):
    smem = pl.BlockSpec(memory_space=pltpu.SMEM)
    vmem = pl.BlockSpec(memory_space=pltpu.VMEM)
    return pl.pallas_call(
        slots_kernel,
        out_shape=jax.ShapeDtypeStruct(ext.shape, BF16),
        in_specs=[smem] * 3 + [vmem] * 5,
        out_specs=vmem,
        compiler_params=pltpu.CompilerParams(vmem_limit_bytes=32 * MIB),
    )(offsets, starts, counts, ext, probe, patterns, *tables)


def reduce_kernel(
    tiles, angles, depth, ids, volume, buf, out,
    near, near_below, below, above, mine, far, plane, own,
    from_left, from_right, send_right, send_left,
    s1, r1, s2, r2, s3, r3, s4, r4, s5, r5, s6, r6, s7, r7,
):
    rows, columns = volume.shape[2:]
    size = reduce_rows
    chunks = rows // size
    core, side, mate, other = slab_partners()
    tile = lax.axis_index("tile")
    angle = lax.axis_index("angle")
    shift = wrapped_shift(ids[0], lax.axis_index("slab"), depth, columns)
    has_next, has_previous = tile < tiles - 1, tile > 0
    has_right, has_left = angle < angles - 1, angle > 0
    left_is_near = angle < angles // 2
    inside = has_left & has_right

    greet_all(pltpu.get_barrier_semaphore(), [
        ("slab", mate, None), ("slab", other, None),
        ("tile", tile - 1, has_previous), ("tile", tile + 1, has_next),
        ("angle", angle - 1, has_left), ("angle", angle + 1, has_right),
    ])

    def part(k, base=0):
        return pl.ds(base + k * size, size)

    parts = (core, 1 - core)

    def wide(ref, k, p):
        return ref[parts[p], part(k)].astype(F32)

    def below_copy(k):
        return remote(
            buf.at[1 - core, part(k, rows)], near_below.at[part(k)], s1.at[k], r1.at[k],
            "slab", mate,
        )

    def near_copy(k):
        return remote(
            buf.at[1 - core, part(k)], near.at[part(k)], s2.at[k], r2.at[k], "slab", mate
        )

    def down_copy(k):
        return remote(below.at[part(k)], above.at[part(k)], s3.at[k], r3.at[k], "tile", tile + 1)

    def far_copy(k):
        return remote(mine.at[part(k)], far.at[part(k)], s4.at[k], r4.at[k], "slab", other)

    def plane_copy(k):
        ref = plane.at[core, part(k)]
        return remote(ref, ref, s5.at[k], r5.at[k], "slab", mate)

    def right_copy(k, p):
        where = (parts[p], part(k))
        return remote(
            send_right.at[where], from_left.at[where], s6.at[p, k], r6.at[p, k],
            "angle", angle + 1,
        )

    def left_copy(k, p):
        where = (parts[p], part(k))
        return remote(
            send_left.at[where], from_right.at[where], s7.at[p, k], r7.at[p, k],
            "angle", angle - 1,
        )

    for k in range(chunks):
        pl.when(has_next)(lambda k=k: below_copy(k).start())
        near_copy(k).start()

    @pl.when(jnp.logical_not(has_previous))
    def _():
        above[...] = jnp.zeros_like(above)

    @pl.when(jnp.logical_not(has_left))
    def _():
        from_left[...] = jnp.zeros_like(from_left)

    @pl.when(jnp.logical_not(has_right))
    def _():
        from_right[...] = jnp.zeros_like(from_right)

    def pass_below(k):
        below_copy(k).wait_recv()
        below[part(k)] = (
            buf[core, part(k, rows)].astype(F32) + near_below[part(k)].astype(F32)
        ).astype(BF16)
        down_copy(k).start()

    def pair_sum(k):
        near_copy(k).wait_recv()
        pl.when(has_previous)(lambda: down_copy(k).wait_recv())
        mine[part(k)] = (
            buf[core, part(k)].astype(F32)
            + near[part(k)].astype(F32)
            + above[part(k)].astype(F32)
        ).astype(BF16)
        far_copy(k).start()

    def slab_sum(k):
        far_copy(k).wait_recv()
        plane[core, part(k)] = (
            mine[part(k)].astype(F32) + far[part(k)].astype(F32)
        ).astype(BF16)
        plane_copy(k).start()
        roll_own(k, 0)

    def mate_sum(k):
        plane_copy(k).wait_recv()
        roll_own(k, 1)

    def roll_own(k, p):
        where = (parts[p], part(k))
        own[where] = pltpu.roll(plane[where].astype(F32), shift, 1)

        @pl.when(jnp.logical_not(has_left) & has_right)
        def _():
            send_right[where] = own[where].astype(BF16)
            right_copy(k, p).start()

        @pl.when(jnp.logical_not(has_right) & has_left)
        def _():
            send_left[where] = own[where].astype(BF16)
            left_copy(k, p).start()

    def move_right(k, p):
        where = (parts[p], part(k))
        right_copy(k, p).wait_recv()

        @pl.when(has_right)
        def _():
            send_right[where] = (own[where] + wide(from_left, k, p)).astype(BF16)
            right_copy(k, p).start()

    def move_left(k, p):
        where = (parts[p], part(k))
        left_copy(k, p).wait_recv()

        @pl.when(has_left)
        def _():
            send_left[where] = (own[where] + wide(from_right, k, p)).astype(BF16)
            left_copy(k, p).start()

    def near_angles(k, p):
        pl.when(left_is_near & has_left)(lambda: move_right(k, p))
        pl.when(jnp.logical_not(left_is_near) & has_right)(lambda: move_left(k, p))

    def far_angles(k, p):
        pl.when(left_is_near & has_right)(lambda: move_left(k, p))
        pl.when(jnp.logical_not(left_is_near) & has_left)(lambda: move_right(k, p))
        total = own[parts[p], part(k)] + wide(from_left, k, p) + wide(from_right, k, p)
        out[parts[p], 0, part(k)] = (
            volume[parts[p], 0, part(k)].astype(F32) - step_size * total
        )

    def inside_far(k, p):
        pl.when(inside)(lambda: far_angles(k, p))

    stages = [
        (0, lambda k: pl.when(has_next)(lambda: pass_below(k))),
        (0, pair_sum), (1, slab_sum), (2, mate_sum),
        (2, lambda k: near_angles(k, 0)), (3, lambda k: near_angles(k, 1)),
        (4, lambda k: inside_far(k, 0)), (5, lambda k: inside_far(k, 1)),
    ]
    for tick in range(chunks + 5):
        for lag, stage in stages:
            if 0 <= tick - lag < chunks:
                stage(tick - lag)

    @pl.when(jnp.logical_not(inside))
    def _():
        for k in range(chunks):
            far_angles(k, 0)
            far_angles(k, 1)

    for k in range(chunks):
        near_copy(k).wait_send()
        far_copy(k).wait_send()
        plane_copy(k).wait_send()

        @pl.when(has_next)
        def _():
            below_copy(k).wait_send()
            down_copy(k).wait_send()

        for p in range(2):
            pl.when(has_right)(lambda: right_copy(k, p).wait_send())
            pl.when(has_left)(lambda: left_copy(k, p).wait_send())


def reduce_update(ids, volume, buf, tiles, angles, depth):
    rows, columns = volume.shape[2:]
    vmem = pl.BlockSpec(memory_space=pltpu.VMEM)
    single = pltpu.VMEM((rows, columns), BF16)
    double = pltpu.VMEM((2, rows, columns), BF16)
    return pl.pallas_call(
        functools.partial(reduce_kernel, tiles, angles, depth),
        out_shape=jax.ShapeDtypeStruct(volume.shape, F32),
        in_specs=[pl.BlockSpec(memory_space=pltpu.SMEM), vmem, vmem],
        out_specs=vmem,
        scratch_shapes=[single] * 6
        + [double, pltpu.VMEM((2, rows, columns), F32)]
        + [double] * 4
        + [pltpu.SemaphoreType.DMA((rows // reduce_rows,))] * 10
        + [pltpu.SemaphoreType.DMA((2, rows // reduce_rows))] * 4,
        compiler_params=pltpu.CompilerParams(
            collective_id=1, has_side_effects=True, vmem_limit_bytes=40 * MIB
        ),
    )(ids, volume, buf)


def per_device(tiles, angles, slabs, volume, probe, amplitudes, offsets, starts, counts, angle_ids):
    width = amplitudes.shape[-1]
    capacity = offsets.shape[3]
    depth = slabs * volume.shape[1]
    ext = project(angle_ids, volume, tiles, depth)
    buf = slots(
        offsets.reshape(capacity), starts.reshape(capacity), counts.reshape(1), ext, probe,
        amplitudes.reshape(capacity, width, width), dft_tables(width),
    )
    return reduce_update(angle_ids, volume, buf, tiles, angles, depth)


def solution(mesh):
    in_specs = (
        P(None, "slab", "tile", None),
        P(),
        P("angle", "tile", "slab", None, None, None),
        P("angle", "tile", "slab", None),
        P("angle", "tile", "slab", None),
        P("angle", "tile", "slab"),
        P("angle"),
    )
    body = functools.partial(
        per_device, mesh.shape["tile"], mesh.shape["angle"], mesh.shape["slab"]
    )
    return jax.shard_map(
        body, mesh=mesh, in_specs=in_specs, out_specs=P(None, "slab", "tile", None),
        check_vma=False,
    )
```

```python
import functools

import jax
import jax.numpy as jnp
import numpy as np
from jax import lax
from jax.experimental import pallas as pl
from jax.experimental.pallas import tpu as pltpu
from jax.sharding import PartitionSpec as P

MESH = pl.DeviceIdType.MESH
BF16 = jnp.bfloat16
F32 = jnp.float32
MIB = 1024 * 1024

angle_center = 600
shear_divisor = 64
step_size = 0.03
floor_square = 0.25
project_rows = 16
reduce_rows = 16


def dft_tables(width):
    line = np.arange(width)
    phase = ((line[:, None] * line[None, :]) % width) * (2.0 * np.pi / width)
    scale = width ** (-0.5)
    return (
        jnp.asarray((np.cos(phase) * scale).astype(np.float32), BF16),
        jnp.asarray((-np.sin(phase) * scale).astype(np.float32), BF16),
    )


def wrapped_shift(angle_value, layer, depth, columns):
    sheared = jnp.right_shift((angle_value - angle_center) * (layer - depth // 2), 6)
    rest = lax.rem(sheared, jnp.int32(columns))
    return jnp.where(rest < 0, rest + columns, rest)


def remote(src, dst, send, recv, axis, index):
    return pltpu.make_async_remote_copy(
        src_ref=src, dst_ref=dst, send_sem=send, recv_sem=recv,
        device_id={axis: index}, device_id_type=MESH,
    )


def slab_partners():
    slab = lax.axis_index("slab")
    core = slab % 2
    side = slab // 2
    return core, side, slab + 1 - 2 * core, slab + 2 - 4 * side


def greet_all(barrier, sides):
    peers = jnp.int32(0)
    for axis, index, here in sides:
        if here is None:
            greet(barrier, axis, index)
            peers += 1
        else:
            pl.when(here)(functools.partial(greet, barrier, axis, index))
            peers += here.astype(jnp.int32)
    pl.semaphore_wait(barrier, peers)


def greet(barrier, axis, index):
    pl.semaphore_signal(barrier, inc=1, device_id={axis: index}, device_id_type=MESH)


def project_kernel(
    tiles, depth, ids, source, ext,
    volume, send, near, half, far, s1, r1, s2, r2, s3, r3, s4, r4, s5, r5, loads,
):
    rows, columns = source.shape[2:]
    chunks = rows // project_rows
    core, side, mate, other = slab_partners()
    tile = lax.axis_index("tile")
    shift = wrapped_shift(ids[0], lax.axis_index("slab"), depth, columns)
    back = lax.rem(columns - shift, jnp.int32(columns))
    parts = (1 - core, core)
    fetched = [
        pltpu.make_async_copy(source.at[parts[i], 0], volume.at[parts[i]], loads.at[i])
        for i in range(2)
    ]
    for copy in fetched:
        copy.start()

    barrier = pltpu.get_barrier_semaphore()
    sides = [
        ("slab", mate, None), ("slab", other, None),
        ("tile", tile - 1, tile > 0), ("tile", tile + 1, tile < tiles - 1),
    ]
    greet_all(barrier, sides)

    def part(k, base=0):
        return pl.ds(base + k * project_rows, project_rows)

    def rolled(index, k):
        return pltpu.roll(volume[index, part(k)].astype(F32), back, 1)

    def first(k):
        return remote(send.at[part(k)], near.at[part(k)], s1, r1.at[k], "slab", mate)

    def second(k):
        return remote(half.at[part(k)], far.at[part(k)], s2, r2.at[k], "slab", other)

    def third(rng):
        return remote(ext.at[core, rng], ext.at[core, rng], s3, r3, "slab", mate)

    def down(k):
        return remote(
            ext.at[core, part(k)], ext.at[core, part(k, rows)], s4, r4.at[k], "tile", tile - 1
        )

    def fifth(rng):
        return remote(ext.at[core, rng], ext.at[core, rng], s5, r5, "slab", mate)

    def start_first(k):
        send[part(k)] = rolled(1 - core, k).astype(BF16)
        first(k).start()

    def start_second(k):
        own = rolled(core, k)
        first(k).wait_recv()
        half[part(k)] = (own + near[part(k)].astype(F32)).astype(BF16)
        second(k).start()

    fetched[0].wait()
    for k in range(2):
        start_first(k)
    fetched[1].wait()
    for k in range(chunks):
        if k + 2 < chunks:
            start_first(k + 2)
        start_second(k)

    for k in range(chunks):
        second(k).wait_recv()
        ext[core, part(k)] = (half[part(k)].astype(F32) + far[part(k)].astype(F32)).astype(BF16)
        pl.when(tile > 0)(lambda: down(k).start())
        third(part(k)).start()

    @pl.when(tile < tiles - 1)
    def _():
        for k in range(chunks):
            down(k).wait_recv()
            fifth(part(k, rows)).start()

    @pl.when(tile == tiles - 1)
    def _():
        ext[:, pl.ds(rows, rows)] = jnp.zeros((2, rows, columns), BF16)

    everything = pl.ds(0, rows)
    remote(send, near, s1, r1.at[0], "slab", mate).wait_send()
    remote(half, far, s2, r2.at[0], "slab", other).wait_send()
    third(everything).wait_send()

    @pl.when(tile > 0)
    def _():
        remote(ext.at[core, everything], far, s4, r4.at[0], "tile", tile - 1).wait_send()

    remote(send, ext.at[1 - core, everything], s1, r3, "slab", mate).wait_recv()

    @pl.when(tile < tiles - 1)
    def _():
        below = pl.ds(rows, rows)
        fifth(below).wait_send()
        remote(send, ext.at[1 - core, below], s1, r5, "slab", mate).wait_recv()


def project(ids, volume, tiles, depth):
    rows, columns = volume.shape[2:]
    vmem = pl.BlockSpec(memory_space=pltpu.VMEM)
    dma = pltpu.SemaphoreType.DMA
    many = dma((rows // project_rows,))
    return pl.pallas_call(
        functools.partial(project_kernel, tiles, depth),
        out_shape=jax.ShapeDtypeStruct((2, 2 * rows, columns), BF16),
        in_specs=[
            pl.BlockSpec(memory_space=pltpu.SMEM), pl.BlockSpec(memory_space=pltpu.HBM)
        ],
        out_specs=vmem,
        scratch_shapes=[pltpu.VMEM((2, rows, columns), BF16)]
        + [pltpu.VMEM((rows, columns), BF16)] * 4
        + [dma, many, dma, many, dma, dma, dma, many, dma, dma]
        + [dma((2,))],
        compiler_params=pltpu.CompilerParams(
            collective_id=0, has_side_effects=True, vmem_limit_bytes=24 * MIB
        ),
    )(ids, volume)


def dot(left, right):
    return jnp.dot(left, right, preferred_element_type=F32)


def sine_cosine(angle):
    turns = jnp.floor(angle * (2.0 / np.pi) + 0.5)
    rest = ((angle - turns * 1.5703125) - turns * 4.837512969970703e-4) - turns * 7.5497899548918e-8
    square = rest * rest
    sine = rest + rest * square * (
        -1.0 / 6 + square * (1.0 / 120 + square * (-1.0 / 5040 + square * (1.0 / 362880)))
    )
    cosine = 1.0 + square * (
        -0.5 + square * (1.0 / 24 + square * (-1.0 / 720 + square * (1.0 / 40320)))
    )
    quadrant = turns.astype(jnp.int32)
    odd = (quadrant & 1) != 0
    found_sine, found_cosine = jnp.where(odd, cosine, sine), jnp.where(odd, sine, cosine)
    return (
        jnp.where((quadrant & 2) != 0, -found_sine, found_sine),
        jnp.where(((quadrant + 1) & 2) != 0, -found_cosine, found_cosine),
    )


def patch_gradient(phase, absorb, probe_real, probe_imag, pattern, table_real, table_imag):
    mag = jnp.exp(-absorb)
    sine, cosine = sine_cosine(phase)
    trans_real = mag * cosine
    trans_imag = mag * sine
    wave_real = (probe_real * trans_real - probe_imag * trans_imag).astype(BF16)
    wave_imag = (probe_real * trans_imag + probe_imag * trans_real).astype(BF16)
    join = functools.partial(jnp.concatenate, axis=0)
    beside = functools.partial(jnp.concatenate, axis=1)
    minus_imag = -table_imag
    rows_forward, columns_forward = beside([table_real, minus_imag]), join([table_real, minus_imag])
    columns_cross = join([table_imag, table_real])
    left_real = dot(rows_forward, join([wave_real, wave_imag])).astype(BF16)
    left_imag = dot(rows_forward, join([wave_imag, -wave_real])).astype(BF16)
    left = beside([left_real, left_imag])
    far_real = dot(left, columns_forward)
    far_imag = dot(left, columns_cross)
    keeping = 1.0 - pattern * lax.rsqrt(far_real * far_real + far_imag * far_imag + floor_square)
    resid_real = (far_real * keeping).astype(BF16)
    resid_imag = (far_imag * keeping).astype(BF16)
    rows_back = beside([table_real, table_imag])
    back_real = dot(rows_back, join([resid_real, resid_imag])).astype(BF16)
    back_imag = dot(rows_back, join([resid_imag, -resid_real])).astype(BF16)
    exit_real = dot(beside([back_real, back_imag]), join([table_real, table_imag]))
    exit_imag = dot(beside([back_imag, back_real]), columns_forward)
    mixed_real = probe_real * exit_real + probe_imag * exit_imag
    mixed_imag = probe_real * exit_imag - probe_imag * exit_real
    final_real = trans_real * mixed_real + trans_imag * mixed_imag
    final_imag = trans_real * mixed_imag - trans_imag * mixed_real
    return final_imag, -final_real


def slots_kernel(offsets, starts, counts, ext, probe, patterns, tr, ti, out):
    width = patterns.shape[-1]
    tall, wide = width + 16, width + 128
    rows, columns = ext.shape[1:]
    out[...] = jnp.zeros_like(out)

    def place(slot):
        r, q = offsets[slot], starts[slot]
        r0 = pl.multiple_of(jnp.minimum((r // 16) * 16, rows - tall), 16)
        q0 = pl.multiple_of(jnp.minimum((q // 128) * 128, columns - wide), 128)
        return r - r0, q - q0, (pl.ds(r0, tall), pl.ds(q0, wide))

    def slot_gradient(slot):
        dr, dq, block = place(slot)

        def window(index):
            raw = ext[(index,) + block].astype(F32)
            raw = pltpu.roll(raw, lax.rem(wide - dq, wide), 1)[:, :width]
            return pltpu.roll(raw, lax.rem(tall - dr, tall), 0)[:width]

        grads = patch_gradient(
            window(0), window(1), probe[0], probe[1], patterns[slot].astype(F32), tr[...], ti[...]
        )
        moved = []
        for index in range(2):
            padded = jnp.concatenate([grads[index], jnp.zeros((16, width), F32)], axis=0)
            padded = pltpu.roll(padded, dr, 0)
            padded = jnp.concatenate([padded, jnp.zeros((tall, 128), F32)], axis=1)
            moved.append(pltpu.roll(padded, dq, 1))
        return moved

    def visit(live):
        found = [slot_gradient(slot) for slot in range(live)]
        for slot in range(live):
            block = place(slot)[2]
            for index in range(2):
                padded = found[slot][index] + out[(index,) + block].astype(F32)
                out[(index,) + block] = padded.astype(BF16)

    for live in range(1, patterns.shape[0] + 1):
        pl.when(counts[0] == live)(functools.partial(visit, live))


def slots(offsets, starts, counts, ext, probe, patterns, tables):
    smem = pl.BlockSpec(memory_space=pltpu.SMEM)
    vmem = pl.BlockSpec(memory_space=pltpu.VMEM)
    return pl.pallas_call(
        slots_kernel,
        out_shape=jax.ShapeDtypeStruct(ext.shape, BF16),
        in_specs=[smem] * 3 + [vmem] * 5,
        out_specs=vmem,
        compiler_params=pltpu.CompilerParams(vmem_limit_bytes=32 * MIB),
    )(offsets, starts, counts, ext, probe, patterns, *tables)


def reduce_kernel(
    tiles, angles, depth, ids, volume, buf, out,
    near, near_below, below, above, mine, far, plane, own,
    from_left, from_right, send_right, send_left,
    s1, r1, s2, r2, s3, r3, s4, r4, s5, r5, s6, r6, s7, r7,
):
    rows, columns = volume.shape[2:]
    size = reduce_rows
    chunks = rows // size
    core, side, mate, other = slab_partners()
    tile = lax.axis_index("tile")
    angle = lax.axis_index("angle")
    shift = wrapped_shift(ids[0], lax.axis_index("slab"), depth, columns)
    has_next, has_previous = tile < tiles - 1, tile > 0
    has_right, has_left = angle < angles - 1, angle > 0
    left_is_near = angle < angles // 2
    inside = has_left & has_right

    greet_all(pltpu.get_barrier_semaphore(), [
        ("slab", mate, None), ("slab", other, None),
        ("tile", tile - 1, has_previous), ("tile", tile + 1, has_next),
        ("angle", angle - 1, has_left), ("angle", angle + 1, has_right),
    ])

    def part(k, base=0):
        return pl.ds(base + k * size, size)

    parts = (core, 1 - core)

    def wide(ref, k, p):
        return ref[parts[p], part(k)].astype(F32)

    def below_copy(k):
        return remote(
            buf.at[1 - core, part(k, rows)], near_below.at[part(k)], s1, r1.at[k],
            "slab", mate,
        )

    def near_copy(k):
        return remote(
            buf.at[1 - core, part(k)], near.at[part(k)], s2, r2.at[k], "slab", mate
        )

    def down_copy(k):
        return remote(below.at[part(k)], above.at[part(k)], s3, r3.at[k], "tile", tile + 1)

    def far_copy(k):
        return remote(mine.at[part(k)], far.at[part(k)], s4, r4.at[k], "slab", other)

    def plane_copy(k):
        ref = plane.at[core, part(k)]
        return remote(ref, ref, s5, r5.at[k], "slab", mate)

    def right_copy(k, p):
        where = (parts[p], part(k))
        return remote(
            send_right.at[where], from_left.at[where], s6, r6.at[p, k],
            "angle", angle + 1,
        )

    def left_copy(k, p):
        where = (parts[p], part(k))
        return remote(
            send_left.at[where], from_right.at[where], s7, r7.at[p, k],
            "angle", angle - 1,
        )

    def start_near(k):
        pl.when(has_next)(lambda: below_copy(k).start())
        near_copy(k).start()

    start_near(0)
    start_near(1)

    @pl.when(jnp.logical_not(has_previous))
    def _():
        above[...] = jnp.zeros_like(above)

    @pl.when(jnp.logical_not(has_left))
    def _():
        from_left[...] = jnp.zeros_like(from_left)

    @pl.when(jnp.logical_not(has_right))
    def _():
        from_right[...] = jnp.zeros_like(from_right)

    def pass_below(k):
        below_copy(k).wait_recv()
        below[part(k)] = (
            buf[core, part(k, rows)].astype(F32) + near_below[part(k)].astype(F32)
        ).astype(BF16)
        down_copy(k).start()

    def pair_sum(k):
        near_copy(k).wait_recv()
        pl.when(has_previous)(lambda: down_copy(k).wait_recv())
        mine[part(k)] = (
            buf[core, part(k)].astype(F32)
            + near[part(k)].astype(F32)
            + above[part(k)].astype(F32)
        ).astype(BF16)
        far_copy(k).start()

    def slab_sum(k):
        far_copy(k).wait_recv()
        plane[core, part(k)] = (
            mine[part(k)].astype(F32) + far[part(k)].astype(F32)
        ).astype(BF16)
        plane_copy(k).start()
        roll_own(k, 0)

    def mate_sum(k):
        plane_copy(k).wait_recv()
        roll_own(k, 1)

    def roll_own(k, p):
        where = (parts[p], part(k))
        own[where] = pltpu.roll(plane[where].astype(F32), shift, 1)

        @pl.when(jnp.logical_not(has_left) & has_right)
        def _():
            send_right[where] = own[where].astype(BF16)
            right_copy(k, p).start()

        @pl.when(jnp.logical_not(has_right) & has_left)
        def _():
            send_left[where] = own[where].astype(BF16)
            left_copy(k, p).start()

    def move_right(k, p):
        where = (parts[p], part(k))
        right_copy(k, p).wait_recv()

        @pl.when(has_right)
        def _():
            send_right[where] = (own[where] + wide(from_left, k, p)).astype(BF16)
            right_copy(k, p).start()

    def move_left(k, p):
        where = (parts[p], part(k))
        left_copy(k, p).wait_recv()

        @pl.when(has_left)
        def _():
            send_left[where] = (own[where] + wide(from_right, k, p)).astype(BF16)
            left_copy(k, p).start()

    def near_angles(k, p):
        pl.when(left_is_near & has_left)(lambda: move_right(k, p))
        pl.when(jnp.logical_not(left_is_near) & has_right)(lambda: move_left(k, p))

    def far_angles(k, p):
        pl.when(left_is_near & has_right)(lambda: move_left(k, p))
        pl.when(jnp.logical_not(left_is_near) & has_left)(lambda: move_right(k, p))
        total = own[parts[p], part(k)] + wide(from_left, k, p) + wide(from_right, k, p)
        out[parts[p], 0, part(k)] = (
            volume[parts[p], 0, part(k)].astype(F32) - step_size * total
        )

    def inside_far(k, p):
        pl.when(inside)(lambda: far_angles(k, p))

    stages = [
        (-2, start_near), (0, lambda k: pl.when(has_next)(lambda: pass_below(k))),
        (0, pair_sum), (1, slab_sum), (2, mate_sum),
        (2, lambda k: near_angles(k, 0)), (3, lambda k: near_angles(k, 1)),
        (4, lambda k: inside_far(k, 0)), (5, lambda k: inside_far(k, 1)),
    ]
    for tick in range(chunks + 5):
        for lag, stage in stages:
            if 0 <= tick - lag < chunks:
                stage(tick - lag)

    @pl.when(jnp.logical_not(inside))
    def _():
        for k in range(chunks):
            far_angles(k, 0)
            far_angles(k, 1)

    everything = pl.ds(0, rows)
    remote(buf.at[1 - core, everything], near, s2, r2.at[0], "slab", mate).wait_send()
    remote(mine, far, s4, r4.at[0], "slab", other).wait_send()
    remote(plane.at[core], plane.at[core], s5, r5.at[0], "slab", mate).wait_send()

    @pl.when(has_next)
    def _():
        remote(
            buf.at[1 - core, pl.ds(rows, rows)], near_below, s1, r1.at[0], "slab", mate
        ).wait_send()
        remote(below, above, s3, r3.at[0], "tile", tile + 1).wait_send()

    @pl.when(has_right)
    def _():
        remote(send_right, from_left, s6, r6.at[0, 0], "angle", angle + 1).wait_send()

    @pl.when(has_left)
    def _():
        remote(send_left, from_right, s7, r7.at[0, 0], "angle", angle - 1).wait_send()


def reduce_update(ids, volume, buf, tiles, angles, depth):
    rows, columns = volume.shape[2:]
    vmem = pl.BlockSpec(memory_space=pltpu.VMEM)
    dma = pltpu.SemaphoreType.DMA
    many = dma((rows // reduce_rows,))
    single = pltpu.VMEM((rows, columns), BF16)
    double = pltpu.VMEM((2, rows, columns), BF16)
    return pl.pallas_call(
        functools.partial(reduce_kernel, tiles, angles, depth),
        out_shape=jax.ShapeDtypeStruct(volume.shape, F32),
        in_specs=[pl.BlockSpec(memory_space=pltpu.SMEM), vmem, vmem],
        out_specs=vmem,
        scratch_shapes=[single] * 6
        + [double, pltpu.VMEM((2, rows, columns), F32)]
        + [double] * 4
        + [dma, many] * 5
        + [dma, dma((2, rows // reduce_rows))] * 2,
        compiler_params=pltpu.CompilerParams(
            collective_id=1, has_side_effects=True, vmem_limit_bytes=40 * MIB
        ),
    )(ids, volume, buf)


def per_device(tiles, angles, slabs, volume, probe, amplitudes, offsets, starts, counts, angle_ids):
    width = amplitudes.shape[-1]
    capacity = offsets.shape[3]
    depth = slabs * volume.shape[1]
    ext = project(angle_ids, volume, tiles, depth)
    buf = slots(
        offsets.reshape(capacity), starts.reshape(capacity), counts.reshape(1), ext, probe,
        amplitudes.reshape(capacity, width, width), dft_tables(width),
    )
    return reduce_update(angle_ids, volume, buf, tiles, angles, depth)


def solution(mesh):
    in_specs = (
        P(None, "slab", "tile", None),
        P(),
        P("angle", "tile", "slab", None, None, None),
        P("angle", "tile", "slab", None),
        P("angle", "tile", "slab", None),
        P("angle", "tile", "slab"),
        P("angle"),
    )
    body = functools.partial(
        per_device, mesh.shape["tile"], mesh.shape["angle"], mesh.shape["slab"]
    )
    return jax.shard_map(
        body, mesh=mesh, in_specs=in_specs, out_specs=P(None, "slab", "tile", None),
        check_vma=False,
    )
```

```python
import functools

import jax
import jax.numpy as jnp
import numpy as np
from jax import lax
from jax.experimental import pallas as pl
from jax.experimental.pallas import tpu as pltpu
from jax.sharding import PartitionSpec as P

MESH = pl.DeviceIdType.MESH
BF16 = jnp.bfloat16
F32 = jnp.float32
MIB = 1024 * 1024

angle_center = 600
shear_divisor = 64
step_size = 0.03
floor_square = 0.25
project_rows = 16
reduce_rows = 16


def dft_tables(width):
    line = np.arange(width)
    phase = ((line[:, None] * line[None, :]) % width) * (2.0 * np.pi / width)
    scale = width ** (-0.5)
    return (
        jnp.asarray((np.cos(phase) * scale).astype(np.float32), BF16),
        jnp.asarray((-np.sin(phase) * scale).astype(np.float32), BF16),
    )


def wrapped_shift(angle_value, layer, depth, columns):
    sheared = jnp.right_shift((angle_value - angle_center) * (layer - depth // 2), 6)
    rest = lax.rem(sheared, jnp.int32(columns))
    return jnp.where(rest < 0, rest + columns, rest)


def remote(src, dst, send, recv, axis, index):
    return pltpu.make_async_remote_copy(
        src_ref=src, dst_ref=dst, send_sem=send, recv_sem=recv,
        device_id={axis: index}, device_id_type=MESH,
    )


def slab_partners():
    slab = lax.axis_index("slab")
    core = slab % 2
    side = slab // 2
    return core, side, slab + 1 - 2 * core, slab + 2 - 4 * side


def greet_all(barrier, sides):
    peers = jnp.int32(0)
    for axis, index, here in sides:
        if here is None:
            greet(barrier, axis, index)
            peers += 1
        else:
            pl.when(here)(functools.partial(greet, barrier, axis, index))
            peers += here.astype(jnp.int32)
    pl.semaphore_wait(barrier, peers)


def greet(barrier, axis, index):
    pl.semaphore_signal(barrier, inc=1, device_id={axis: index}, device_id_type=MESH)


def project_kernel(
    tiles, depth, ids, source, ext,
    volume, send, near, half, far, s1, r1, s2, r2, s3, r3, s4, r4, s5, r5, loads,
):
    rows, columns = source.shape[2:]
    chunks = rows // project_rows
    core, side, mate, other = slab_partners()
    tile = lax.axis_index("tile")
    shift = wrapped_shift(ids[0], lax.axis_index("slab"), depth, columns)
    back = lax.rem(columns - shift, jnp.int32(columns))
    parts = (1 - core, core)
    fetched = [
        pltpu.make_async_copy(source.at[parts[i], 0], volume.at[parts[i]], loads.at[i])
        for i in range(2)
    ]
    for copy in fetched:
        copy.start()

    barrier = pltpu.get_barrier_semaphore()
    sides = [
        ("slab", mate, None), ("slab", other, None),
        ("tile", tile - 1, tile > 0), ("tile", tile + 1, tile < tiles - 1),
    ]
    greet_all(barrier, sides)

    def part(k, base=0):
        return pl.ds(base + k * project_rows, project_rows)

    def rolled(index, k):
        return pltpu.roll(volume[index, part(k)].astype(F32), back, 1)

    def first(k):
        return remote(send.at[part(k)], near.at[part(k)], s1, r1.at[k], "slab", mate)

    def second(k):
        return remote(half.at[part(k)], far.at[part(k)], s2, r2.at[k], "slab", other)

    def third(rng):
        return remote(ext.at[core, rng], ext.at[core, rng], s3, r3, "slab", mate)

    def down(k):
        return remote(
            ext.at[core, part(k)], ext.at[core, part(k, rows)], s4, r4.at[k], "tile", tile - 1
        )

    def fifth(rng):
        return remote(ext.at[core, rng], ext.at[core, rng], s5, r5, "slab", mate)

    def start_first(k):
        send[part(k)] = rolled(1 - core, k).astype(BF16)
        first(k).start()

    def start_second(k):
        own = rolled(core, k)
        first(k).wait_recv()
        half[part(k)] = (own + near[part(k)].astype(F32)).astype(BF16)
        second(k).start()

    fetched[0].wait()
    for k in range(2):
        start_first(k)
    fetched[1].wait()

    def finish(k):
        second(k).wait_recv()
        ext[core, part(k)] = (half[part(k)].astype(F32) + far[part(k)].astype(F32)).astype(BF16)
        pl.when(tile > 0)(lambda: down(k).start())
        third(part(k)).start()

    for k in range(chunks + 3):
        if k + 2 < chunks:
            start_first(k + 2)
        if k < chunks:
            start_second(k)
        if k >= 3:
            finish(k - 3)

    @pl.when(tile < tiles - 1)
    def _():
        for k in range(chunks):
            down(k).wait_recv()
            fifth(part(k, rows)).start()

    @pl.when(tile == tiles - 1)
    def _():
        ext[:, pl.ds(rows, rows)] = jnp.zeros((2, rows, columns), BF16)

    everything = pl.ds(0, rows)
    remote(send, near, s1, r1.at[0], "slab", mate).wait_send()
    remote(half, far, s2, r2.at[0], "slab", other).wait_send()
    third(everything).wait_send()

    @pl.when(tile > 0)
    def _():
        remote(ext.at[core, everything], far, s4, r4.at[0], "tile", tile - 1).wait_send()

    remote(send, ext.at[1 - core, everything], s1, r3, "slab", mate).wait_recv()

    @pl.when(tile < tiles - 1)
    def _():
        below = pl.ds(rows, rows)
        fifth(below).wait_send()
        remote(send, ext.at[1 - core, below], s1, r5, "slab", mate).wait_recv()


def project(ids, volume, tiles, depth):
    rows, columns = volume.shape[2:]
    vmem = pl.BlockSpec(memory_space=pltpu.VMEM)
    dma = pltpu.SemaphoreType.DMA
    many = dma((rows // project_rows,))
    return pl.pallas_call(
        functools.partial(project_kernel, tiles, depth),
        out_shape=jax.ShapeDtypeStruct((2, 2 * rows, columns), BF16),
        in_specs=[
            pl.BlockSpec(memory_space=pltpu.SMEM), pl.BlockSpec(memory_space=pltpu.HBM)
        ],
        out_specs=vmem,
        scratch_shapes=[pltpu.VMEM((2, rows, columns), BF16)]
        + [pltpu.VMEM((rows, columns), BF16)] * 4
        + [dma, many, dma, many, dma, dma, dma, many, dma, dma]
        + [dma((2,))],
        compiler_params=pltpu.CompilerParams(
            collective_id=0, has_side_effects=True, vmem_limit_bytes=24 * MIB
        ),
    )(ids, volume)


def dot(left, right):
    return jnp.dot(left, right, preferred_element_type=F32)


def sine_cosine(angle):
    turns = jnp.floor(angle * (2.0 / np.pi) + 0.5)
    rest = ((angle - turns * 1.5703125) - turns * 4.837512969970703e-4) - turns * 7.5497899548918e-8
    square = rest * rest
    sine = rest + rest * square * (
        -1.0 / 6 + square * (1.0 / 120 + square * (-1.0 / 5040 + square * (1.0 / 362880)))
    )
    cosine = 1.0 + square * (
        -0.5 + square * (1.0 / 24 + square * (-1.0 / 720 + square * (1.0 / 40320)))
    )
    quadrant = turns.astype(jnp.int32)
    odd = (quadrant & 1) != 0
    found_sine, found_cosine = jnp.where(odd, cosine, sine), jnp.where(odd, sine, cosine)
    return (
        jnp.where((quadrant & 2) != 0, -found_sine, found_sine),
        jnp.where(((quadrant + 1) & 2) != 0, -found_cosine, found_cosine),
    )


def patch_gradient(phase, absorb, probe_real, probe_imag, pattern, table_real, table_imag):
    mag = jnp.exp(-absorb)
    sine, cosine = sine_cosine(phase)
    trans_real = mag * cosine
    trans_imag = mag * sine
    wave_real = (probe_real * trans_real - probe_imag * trans_imag).astype(BF16)
    wave_imag = (probe_real * trans_imag + probe_imag * trans_real).astype(BF16)
    join = functools.partial(jnp.concatenate, axis=0)
    beside = functools.partial(jnp.concatenate, axis=1)
    minus_imag = -table_imag
    rows_forward, columns_forward = beside([table_real, minus_imag]), join([table_real, minus_imag])
    columns_cross = join([table_imag, table_real])
    left_real = dot(rows_forward, join([wave_real, wave_imag])).astype(BF16)
    left_imag = dot(rows_forward, join([wave_imag, -wave_real])).astype(BF16)
    left = beside([left_real, left_imag])
    far_real = dot(left, columns_forward)
    far_imag = dot(left, columns_cross)
    keeping = 1.0 - pattern * lax.rsqrt(far_real * far_real + far_imag * far_imag + floor_square)
    resid_real = (far_real * keeping).astype(BF16)
    resid_imag = (far_imag * keeping).astype(BF16)
    rows_back = beside([table_real, table_imag])
    back_real = dot(rows_back, join([resid_real, resid_imag])).astype(BF16)
    back_imag = dot(rows_back, join([resid_imag, -resid_real])).astype(BF16)
    exit_real = dot(beside([back_real, back_imag]), join([table_real, table_imag]))
    exit_imag = dot(beside([back_imag, back_real]), columns_forward)
    mixed_real = probe_real * exit_real + probe_imag * exit_imag
    mixed_imag = probe_real * exit_imag - probe_imag * exit_real
    final_real = trans_real * mixed_real + trans_imag * mixed_imag
    final_imag = trans_real * mixed_imag - trans_imag * mixed_real
    return final_imag, -final_real


def slots_kernel(offsets, starts, counts, ext, probe, patterns, tr, ti, out):
    width = patterns.shape[-1]
    tall, wide = width + 16, width + 128
    rows, columns = ext.shape[1:]
    out[...] = jnp.zeros_like(out)

    def place(slot):
        r, q = offsets[slot], starts[slot]
        r0 = pl.multiple_of(jnp.minimum((r // 16) * 16, rows - tall), 16)
        q0 = pl.multiple_of(jnp.minimum((q // 128) * 128, columns - wide), 128)
        return r - r0, q - q0, (pl.ds(r0, tall), pl.ds(q0, wide))

    def slot_gradient(slot):
        dr, dq, block = place(slot)

        def window(index):
            raw = ext[(index,) + block].astype(F32)
            raw = pltpu.roll(raw, lax.rem(wide - dq, wide), 1)[:, :width]
            return pltpu.roll(raw, lax.rem(tall - dr, tall), 0)[:width]

        grads = patch_gradient(
            window(0), window(1), probe[0], probe[1], patterns[slot].astype(F32), tr[...], ti[...]
        )
        moved = []
        for index in range(2):
            padded = jnp.concatenate([grads[index], jnp.zeros((16, width), F32)], axis=0)
            padded = pltpu.roll(padded, dr, 0)
            padded = jnp.concatenate([padded, jnp.zeros((tall, 128), F32)], axis=1)
            moved.append(pltpu.roll(padded, dq, 1))
        return moved

    def visit(live):
        found = [slot_gradient(slot) for slot in range(live)]
        for slot in range(live):
            block = place(slot)[2]
            for index in range(2):
                padded = found[slot][index] + out[(index,) + block].astype(F32)
                out[(index,) + block] = padded.astype(BF16)

    for live in range(1, patterns.shape[0] + 1):
        pl.when(counts[0] == live)(functools.partial(visit, live))


def slots(offsets, starts, counts, ext, probe, patterns, tables):
    smem = pl.BlockSpec(memory_space=pltpu.SMEM)
    vmem = pl.BlockSpec(memory_space=pltpu.VMEM)
    return pl.pallas_call(
        slots_kernel,
        out_shape=jax.ShapeDtypeStruct(ext.shape, BF16),
        in_specs=[smem] * 3 + [vmem] * 5,
        out_specs=vmem,
        compiler_params=pltpu.CompilerParams(vmem_limit_bytes=32 * MIB),
    )(offsets, starts, counts, ext, probe, patterns, *tables)


def reduce_kernel(
    tiles, angles, depth, ids, volume, buf, out,
    near, near_below, below, above, mine, far, plane, own,
    from_left, from_right, send_right, send_left,
    s1, r1, s2, r2, s3, r3, s4, r4, s5, r5, s6, r6, s7, r7,
):
    rows, columns = volume.shape[2:]
    size = reduce_rows
    chunks = rows // size
    core, side, mate, other = slab_partners()
    tile = lax.axis_index("tile")
    angle = lax.axis_index("angle")
    shift = wrapped_shift(ids[0], lax.axis_index("slab"), depth, columns)
    has_next, has_previous = tile < tiles - 1, tile > 0
    has_right, has_left = angle < angles - 1, angle > 0
    left_is_near = angle < angles // 2
    inside = has_left & has_right

    greet_all(pltpu.get_barrier_semaphore(), [
        ("slab", mate, None), ("slab", other, None),
        ("tile", tile - 1, has_previous), ("tile", tile + 1, has_next),
        ("angle", angle - 1, has_left), ("angle", angle + 1, has_right),
    ])

    def part(k, base=0):
        return pl.ds(base + k * size, size)

    parts = (core, 1 - core)

    def wide(ref, k, p):
        return ref[parts[p], part(k)].astype(F32)

    def below_copy(k):
        return remote(
            buf.at[1 - core, part(k, rows)], near_below.at[part(k)], s1, r1.at[k],
            "slab", mate,
        )

    def near_copy(k):
        return remote(
            buf.at[1 - core, part(k)], near.at[part(k)], s2, r2.at[k], "slab", mate
        )

    def down_copy(k):
        return remote(below.at[part(k)], above.at[part(k)], s3, r3.at[k], "tile", tile + 1)

    def far_copy(k):
        return remote(mine.at[part(k)], far.at[part(k)], s4, r4.at[k], "slab", other)

    def plane_copy(k):
        ref = plane.at[core, part(k)]
        return remote(ref, ref, s5, r5.at[k], "slab", mate)

    def right_copy(k, p):
        where = (parts[p], part(k))
        return remote(
            send_right.at[where], from_left.at[where], s6, r6.at[p, k],
            "angle", angle + 1,
        )

    def left_copy(k, p):
        where = (parts[p], part(k))
        return remote(
            send_left.at[where], from_right.at[where], s7, r7.at[p, k],
            "angle", angle - 1,
        )

    def start_near(k):
        pl.when(has_next)(lambda: below_copy(k).start())
        near_copy(k).start()

    start_near(0)
    start_near(1)

    @pl.when(jnp.logical_not(has_previous))
    def _():
        above[...] = jnp.zeros_like(above)

    @pl.when(jnp.logical_not(has_left))
    def _():
        from_left[...] = jnp.zeros_like(from_left)

    @pl.when(jnp.logical_not(has_right))
    def _():
        from_right[...] = jnp.zeros_like(from_right)

    def pass_below(k):
        below_copy(k).wait_recv()
        below[part(k)] = (
            buf[core, part(k, rows)].astype(F32) + near_below[part(k)].astype(F32)
        ).astype(BF16)
        down_copy(k).start()

    def pair_sum(k):
        near_copy(k).wait_recv()
        pl.when(has_previous)(lambda: down_copy(k).wait_recv())
        mine[part(k)] = (
            buf[core, part(k)].astype(F32)
            + near[part(k)].astype(F32)
            + above[part(k)].astype(F32)
        ).astype(BF16)
        far_copy(k).start()

    def slab_sum(k):
        far_copy(k).wait_recv()
        plane[core, part(k)] = (
            mine[part(k)].astype(F32) + far[part(k)].astype(F32)
        ).astype(BF16)
        plane_copy(k).start()
        roll_own(k, 0)

    def mate_sum(k):
        plane_copy(k).wait_recv()
        roll_own(k, 1)

    def roll_own(k, p):
        where = (parts[p], part(k))
        own[where] = pltpu.roll(plane[where].astype(F32), shift, 1)

        @pl.when(jnp.logical_not(has_left) & has_right)
        def _():
            send_right[where] = own[where].astype(BF16)
            right_copy(k, p).start()

        @pl.when(jnp.logical_not(has_right) & has_left)
        def _():
            send_left[where] = own[where].astype(BF16)
            left_copy(k, p).start()

    def move_right(k, p):
        where = (parts[p], part(k))
        right_copy(k, p).wait_recv()

        @pl.when(has_right)
        def _():
            send_right[where] = (own[where] + wide(from_left, k, p)).astype(BF16)
            right_copy(k, p).start()

    def move_left(k, p):
        where = (parts[p], part(k))
        left_copy(k, p).wait_recv()

        @pl.when(has_left)
        def _():
            send_left[where] = (own[where] + wide(from_right, k, p)).astype(BF16)
            left_copy(k, p).start()

    def near_angles(k, p):
        pl.when(left_is_near & has_left)(lambda: move_right(k, p))
        pl.when(jnp.logical_not(left_is_near) & has_right)(lambda: move_left(k, p))

    def far_angles(k, p):
        pl.when(left_is_near & has_right)(lambda: move_left(k, p))
        pl.when(jnp.logical_not(left_is_near) & has_left)(lambda: move_right(k, p))
        total = own[parts[p], part(k)] + wide(from_left, k, p) + wide(from_right, k, p)
        out[parts[p], 0, part(k)] = (
            volume[parts[p], 0, part(k)].astype(F32) - step_size * total
        )

    def inside_far(k, p):
        pl.when(inside)(lambda: far_angles(k, p))

    stages = [
        (-3, start_near), (-1, lambda k: pl.when(has_next)(lambda: pass_below(k))),
        (0, pair_sum), (1, slab_sum), (2, mate_sum),
        (2, lambda k: near_angles(k, 0)), (3, lambda k: near_angles(k, 1)),
        (4, lambda k: inside_far(k, 0)), (5, lambda k: inside_far(k, 1)),
    ]
    for tick in range(-1, chunks + 5):
        for lag, stage in stages:
            if 0 <= tick - lag < chunks:
                stage(tick - lag)

    @pl.when(jnp.logical_not(inside))
    def _():
        for k in range(chunks):
            far_angles(k, 0)
            far_angles(k, 1)

    everything = pl.ds(0, rows)
    remote(buf.at[1 - core, everything], near, s2, r2.at[0], "slab", mate).wait_send()
    remote(mine, far, s4, r4.at[0], "slab", other).wait_send()
    remote(plane.at[core], plane.at[core], s5, r5.at[0], "slab", mate).wait_send()

    @pl.when(has_next)
    def _():
        remote(
            buf.at[1 - core, pl.ds(rows, rows)], near_below, s1, r1.at[0], "slab", mate
        ).wait_send()
        remote(below, above, s3, r3.at[0], "tile", tile + 1).wait_send()

    @pl.when(has_right)
    def _():
        remote(send_right, from_left, s6, r6.at[0, 0], "angle", angle + 1).wait_send()

    @pl.when(has_left)
    def _():
        remote(send_left, from_right, s7, r7.at[0, 0], "angle", angle - 1).wait_send()


def reduce_update(ids, volume, buf, tiles, angles, depth):
    rows, columns = volume.shape[2:]
    vmem = pl.BlockSpec(memory_space=pltpu.VMEM)
    dma = pltpu.SemaphoreType.DMA
    many = dma((rows // reduce_rows,))
    single = pltpu.VMEM((rows, columns), BF16)
    double = pltpu.VMEM((2, rows, columns), BF16)
    return pl.pallas_call(
        functools.partial(reduce_kernel, tiles, angles, depth),
        out_shape=jax.ShapeDtypeStruct(volume.shape, F32),
        in_specs=[pl.BlockSpec(memory_space=pltpu.SMEM), vmem, vmem],
        out_specs=vmem,
        scratch_shapes=[single] * 6
        + [double, pltpu.VMEM((2, rows, columns), F32)]
        + [double] * 4
        + [dma, many] * 5
        + [dma, dma((2, rows // reduce_rows))] * 2,
        compiler_params=pltpu.CompilerParams(
            collective_id=1, has_side_effects=True, vmem_limit_bytes=40 * MIB
        ),
    )(ids, volume, buf)


def per_device(tiles, angles, slabs, volume, probe, amplitudes, offsets, starts, counts, angle_ids):
    width = amplitudes.shape[-1]
    capacity = offsets.shape[3]
    depth = slabs * volume.shape[1]
    ext = project(angle_ids, volume, tiles, depth)
    buf = slots(
        offsets.reshape(capacity), starts.reshape(capacity), counts.reshape(1), ext, probe,
        amplitudes.reshape(capacity, width, width), dft_tables(width),
    )
    return reduce_update(angle_ids, volume, buf, tiles, angles, depth)


def solution(mesh):
    in_specs = (
        P(None, "slab", "tile", None),
        P(),
        P("angle", "tile", "slab", None, None, None),
        P("angle", "tile", "slab", None),
        P("angle", "tile", "slab", None),
        P("angle", "tile", "slab"),
        P("angle"),
    )
    body = functools.partial(
        per_device, mesh.shape["tile"], mesh.shape["angle"], mesh.shape["slab"]
    )
    return jax.shard_map(
        body, mesh=mesh, in_specs=in_specs, out_specs=P(None, "slab", "tile", None),
        check_vma=False,
    )
```

```python
import functools

import jax
import jax.numpy as jnp
import numpy as np
from jax import lax
from jax.experimental import pallas as pl
from jax.experimental.pallas import tpu as pltpu
from jax.sharding import PartitionSpec as P

MESH = pl.DeviceIdType.MESH
BF16 = jnp.bfloat16
F32 = jnp.float32
MIB = 1024 * 1024

angle_center = 600
shear_divisor = 64
step_size = 0.03
floor_square = 0.25
project_rows = 16
reduce_rows = 16


def dft_tables(width):
    line = np.arange(width)
    phase = ((line[:, None] * line[None, :]) % width) * (2.0 * np.pi / width)
    scale = width ** (-0.5)
    return (
        jnp.asarray((np.cos(phase) * scale).astype(np.float32), BF16),
        jnp.asarray((-np.sin(phase) * scale).astype(np.float32), BF16),
    )


def wrapped_shift(angle_value, layer, depth, columns):
    sheared = jnp.right_shift((angle_value - angle_center) * (layer - depth // 2), 6)
    rest = lax.rem(sheared, jnp.int32(columns))
    return jnp.where(rest < 0, rest + columns, rest)


def remote(src, dst, send, recv, axis, index):
    return pltpu.make_async_remote_copy(
        src_ref=src, dst_ref=dst, send_sem=send, recv_sem=recv,
        device_id={axis: index}, device_id_type=MESH,
    )


def slab_partners():
    slab = lax.axis_index("slab")
    core = slab % 2
    side = slab // 2
    return core, side, slab + 1 - 2 * core, slab + 2 - 4 * side


def greet_all(barrier, sides):
    peers = jnp.int32(0)
    for axis, index, here in sides:
        if here is None:
            greet(barrier, axis, index)
            peers += 1
        else:
            pl.when(here)(functools.partial(greet, barrier, axis, index))
            peers += here.astype(jnp.int32)
    pl.semaphore_wait(barrier, peers)


def greet(barrier, axis, index):
    pl.semaphore_signal(barrier, inc=1, device_id={axis: index}, device_id_type=MESH)


def project_kernel(
    tiles, depth, ids, source, ext,
    volume, send, near, half, far, s1, r1, s2, r2, s3, r3, s4, r4, s5, r5, loads,
):
    rows, columns = source.shape[2:]
    chunks = rows // project_rows
    core, side, mate, other = slab_partners()
    tile = lax.axis_index("tile")
    shift = wrapped_shift(ids[0], lax.axis_index("slab"), depth, columns)
    back = lax.rem(columns - shift, jnp.int32(columns))
    parts = (1 - core, core)
    fetched = [
        pltpu.make_async_copy(source.at[parts[i], 0], volume.at[parts[i]], loads.at[i])
        for i in range(2)
    ]
    for copy in fetched:
        copy.start()

    barrier = pltpu.get_barrier_semaphore()
    sides = [
        ("slab", mate, None), ("slab", other, None),
        ("tile", tile - 1, tile > 0), ("tile", tile + 1, tile < tiles - 1),
    ]
    greet_all(barrier, sides)

    def part(k, base=0):
        return pl.ds(base + k * project_rows, project_rows)

    def rolled(index, k):
        return pltpu.roll(volume[index, part(k)].astype(F32), back, 1)

    def first(k):
        return remote(send.at[part(k)], near.at[part(k)], s1, r1.at[k], "slab", mate)

    def second(k):
        return remote(half.at[part(k)], far.at[part(k)], s2, r2.at[k], "slab", other)

    def third(rng):
        return remote(ext.at[core, rng], ext.at[core, rng], s3, r3, "slab", mate)

    def down(k):
        return remote(
            ext.at[core, part(k)], ext.at[core, part(k, rows)], s4, r4.at[k], "tile", tile - 1
        )

    def fifth(rng):
        return remote(ext.at[core, rng], ext.at[core, rng], s5, r5, "slab", mate)

    def start_first(k):
        send[part(k)] = rolled(1 - core, k).astype(BF16)
        first(k).start()

    def start_second(k):
        own = rolled(core, k)
        first(k).wait_recv()
        half[part(k)] = (own + near[part(k)].astype(F32)).astype(BF16)
        second(k).start()

    fetched[0].wait()
    for k in range(2):
        start_first(k)
    fetched[1].wait()

    def finish(k):
        second(k).wait_recv()
        ext[core, part(k)] = (half[part(k)].astype(F32) + far[part(k)].astype(F32)).astype(BF16)
        pl.when(tile > 0)(lambda: down(k).start())
        third(part(k)).start()

    for k in range(chunks + 3):
        if k + 2 < chunks:
            start_first(k + 2)
        if k < chunks:
            start_second(k)
        if k >= 3:
            finish(k - 3)

    @pl.when(tile < tiles - 1)
    def _():
        for k in range(chunks):
            down(k).wait_recv()
            fifth(part(k, rows)).start()

    @pl.when(tile == tiles - 1)
    def _():
        ext[:, pl.ds(rows, rows)] = jnp.zeros((2, rows, columns), BF16)

    everything = pl.ds(0, rows)
    remote(send, near, s1, r1.at[0], "slab", mate).wait_send()
    remote(half, far, s2, r2.at[0], "slab", other).wait_send()
    third(everything).wait_send()

    @pl.when(tile > 0)
    def _():
        remote(ext.at[core, everything], far, s4, r4.at[0], "tile", tile - 1).wait_send()

    remote(send, ext.at[1 - core, everything], s1, r3, "slab", mate).wait_recv()

    @pl.when(tile < tiles - 1)
    def _():
        below = pl.ds(rows, rows)
        fifth(below).wait_send()
        remote(send, ext.at[1 - core, below], s1, r5, "slab", mate).wait_recv()


def project(ids, volume, tiles, depth):
    rows, columns = volume.shape[2:]
    vmem = pl.BlockSpec(memory_space=pltpu.VMEM)
    dma = pltpu.SemaphoreType.DMA
    many = dma((rows // project_rows,))
    return pl.pallas_call(
        functools.partial(project_kernel, tiles, depth),
        out_shape=jax.ShapeDtypeStruct((2, 2 * rows, columns), BF16),
        in_specs=[
            pl.BlockSpec(memory_space=pltpu.SMEM), pl.BlockSpec(memory_space=pltpu.HBM)
        ],
        out_specs=vmem,
        scratch_shapes=[pltpu.VMEM((2, rows, columns), BF16)]
        + [pltpu.VMEM((rows, columns), BF16)] * 4
        + [dma, many, dma, many, dma, dma, dma, many, dma, dma]
        + [dma((2,))],
        compiler_params=pltpu.CompilerParams(
            collective_id=0, has_side_effects=True, vmem_limit_bytes=24 * MIB
        ),
    )(ids, volume)


def dot(left, right):
    return jnp.dot(left, right, preferred_element_type=F32)


def sine_cosine(angle):
    turns = jnp.floor(angle * (2.0 / np.pi) + 0.5)
    rest = ((angle - turns * 1.5703125) - turns * 4.837512969970703e-4) - turns * 7.5497899548918e-8
    square = rest * rest
    sine = rest + rest * square * (
        -1.0 / 6 + square * (1.0 / 120 + square * (-1.0 / 5040 + square * (1.0 / 362880)))
    )
    cosine = 1.0 + square * (
        -0.5 + square * (1.0 / 24 + square * (-1.0 / 720 + square * (1.0 / 40320)))
    )
    quadrant = turns.astype(jnp.int32)
    odd = (quadrant & 1) != 0
    found_sine, found_cosine = jnp.where(odd, cosine, sine), jnp.where(odd, sine, cosine)
    return (
        jnp.where((quadrant & 2) != 0, -found_sine, found_sine),
        jnp.where(((quadrant + 1) & 2) != 0, -found_cosine, found_cosine),
    )


def patch_gradient(phase, absorb, probe_real, probe_imag, pattern, table_real, table_imag):
    mag = jnp.exp(-absorb)
    sine, cosine = sine_cosine(phase)
    trans_real = mag * cosine
    trans_imag = mag * sine
    wave_real = (probe_real * trans_real - probe_imag * trans_imag).astype(BF16)
    wave_imag = (probe_real * trans_imag + probe_imag * trans_real).astype(BF16)
    join = functools.partial(jnp.concatenate, axis=0)
    beside = functools.partial(jnp.concatenate, axis=1)
    minus_imag = -table_imag
    rows_forward, columns_forward = beside([table_real, minus_imag]), join([table_real, minus_imag])
    columns_cross = join([table_imag, table_real])
    left_real = dot(rows_forward, join([wave_real, wave_imag])).astype(BF16)
    left_imag = dot(rows_forward, join([wave_imag, -wave_real])).astype(BF16)
    left = beside([left_real, left_imag])
    far_real = dot(left, columns_forward)
    far_imag = dot(left, columns_cross)
    keeping = 1.0 - pattern * lax.rsqrt(far_real * far_real + far_imag * far_imag + floor_square)
    resid_real = (far_real * keeping).astype(BF16)
    resid_imag = (far_imag * keeping).astype(BF16)
    rows_back = beside([table_real, table_imag])
    back_real = dot(rows_back, join([resid_real, resid_imag])).astype(BF16)
    back_imag = dot(rows_back, join([resid_imag, -resid_real])).astype(BF16)
    exit_real = dot(beside([back_real, back_imag]), join([table_real, table_imag]))
    exit_imag = dot(beside([back_imag, back_real]), columns_forward)
    mixed_real = probe_real * exit_real + probe_imag * exit_imag
    mixed_imag = probe_real * exit_imag - probe_imag * exit_real
    final_real = trans_real * mixed_real + trans_imag * mixed_imag
    final_imag = trans_real * mixed_imag - trans_imag * mixed_real
    return final_imag, -final_real


def slots_kernel(offsets, starts, counts, ext, probe, patterns, tr, ti, out):
    width = patterns.shape[-1]
    tall, wide = width + 16, width + 128
    rows, columns = ext.shape[1:]
    out[...] = jnp.zeros_like(out)

    def place(slot):
        r, q = offsets[slot], starts[slot]
        r0 = pl.multiple_of(jnp.minimum((r // 16) * 16, rows - tall), 16)
        q0 = pl.multiple_of(jnp.minimum((q // 128) * 128, columns - wide), 128)
        return r - r0, q - q0, (pl.ds(r0, tall), pl.ds(q0, wide))

    def slot_gradient(slot):
        dr, dq, block = place(slot)

        def window(index):
            raw = ext[(index,) + block].astype(F32)
            raw = pltpu.roll(raw, lax.rem(wide - dq, wide), 1)[:, :width]
            return pltpu.roll(raw, lax.rem(tall - dr, tall), 0)[:width]

        grads = patch_gradient(
            window(0), window(1), probe[0], probe[1], patterns[slot].astype(F32), tr[...], ti[...]
        )
        moved = []
        for index in range(2):
            padded = jnp.concatenate([grads[index], jnp.zeros((16, width), F32)], axis=0)
            padded = pltpu.roll(padded, dr, 0)
            padded = jnp.concatenate([padded, jnp.zeros((tall, 128), F32)], axis=1)
            moved.append(pltpu.roll(padded, dq, 1))
        return moved

    def visit(live):
        found = [slot_gradient(slot) for slot in range(live)]
        for slot in range(live):
            block = place(slot)[2]
            for index in range(2):
                padded = found[slot][index] + out[(index,) + block].astype(F32)
                out[(index,) + block] = padded.astype(BF16)

    for live in range(1, patterns.shape[0] + 1):
        pl.when(counts[0] == live)(functools.partial(visit, live))


def slots(offsets, starts, counts, ext, probe, patterns, tables):
    smem = pl.BlockSpec(memory_space=pltpu.SMEM)
    vmem = pl.BlockSpec(memory_space=pltpu.VMEM)
    return pl.pallas_call(
        slots_kernel,
        out_shape=jax.ShapeDtypeStruct(ext.shape, BF16),
        in_specs=[smem] * 3 + [vmem] * 5,
        out_specs=vmem,
        compiler_params=pltpu.CompilerParams(vmem_limit_bytes=32 * MIB),
    )(offsets, starts, counts, ext, probe, patterns, *tables)


def reduce_kernel(
    tiles, angles, depth, ids, volume, buf, out,
    near, near_below, below, above, mine, far, plane, own,
    from_left, from_right, send_right, send_left,
    s1, r1, s2, r2, s3, r3, s4, r4, s5, r5, s6, r6, s7, r7,
):
    rows, columns = volume.shape[2:]
    size = reduce_rows
    chunks = rows // size
    core, side, mate, other = slab_partners()
    tile = lax.axis_index("tile")
    angle = lax.axis_index("angle")
    shift = wrapped_shift(ids[0], lax.axis_index("slab"), depth, columns)
    has_next, has_previous = tile < tiles - 1, tile > 0
    has_right, has_left = angle < angles - 1, angle > 0
    left_is_near = angle < angles // 2
    inside = has_left & has_right

    greet_all(pltpu.get_barrier_semaphore(), [
        ("slab", mate, None), ("slab", other, None),
        ("tile", tile - 1, has_previous), ("tile", tile + 1, has_next),
        ("angle", angle - 1, has_left), ("angle", angle + 1, has_right),
    ])

    def part(k, base=0):
        return pl.ds(base + k * size, size)

    parts = (core, 1 - core)

    def wide(ref, k, p):
        return ref[parts[p], part(k)].astype(F32)

    def below_copy(k):
        return remote(
            buf.at[1 - core, part(k, rows)], near_below.at[part(k)], s1, r1.at[k],
            "slab", mate,
        )

    def near_copy(k):
        return remote(
            buf.at[1 - core, part(k)], near.at[part(k)], s2, r2.at[k], "slab", mate
        )

    def down_copy(k):
        return remote(below.at[part(k)], above.at[part(k)], s3, r3.at[k], "tile", tile + 1)

    def far_copy(k):
        return remote(mine.at[part(k)], far.at[part(k)], s4, r4.at[k], "slab", other)

    def plane_copy(k):
        ref = plane.at[core, part(k)]
        return remote(ref, ref, s5, r5.at[k], "slab", mate)

    def right_copy(k, p):
        where = (parts[p], part(k))
        return remote(
            send_right.at[where], from_left.at[where], s6, r6.at[p, k],
            "angle", angle + 1,
        )

    def left_copy(k, p):
        where = (parts[p], part(k))
        return remote(
            send_left.at[where], from_right.at[where], s7, r7.at[p, k],
            "angle", angle - 1,
        )

    def start_near(k):
        pl.when(has_next)(lambda: below_copy(k).start())
        near_copy(k).start()

    start_near(0)
    start_near(1)

    @pl.when(jnp.logical_not(has_previous))
    def _():
        above[...] = jnp.zeros_like(above)

    @pl.when(jnp.logical_not(has_left))
    def _():
        from_left[...] = jnp.zeros_like(from_left)

    @pl.when(jnp.logical_not(has_right))
    def _():
        from_right[...] = jnp.zeros_like(from_right)

    def pass_below(k):
        below_copy(k).wait_recv()
        below[part(k)] = (
            buf[core, part(k, rows)].astype(F32) + near_below[part(k)].astype(F32)
        ).astype(BF16)
        down_copy(k).start()

    def pair_sum(k):
        near_copy(k).wait_recv()
        pl.when(has_previous)(lambda: down_copy(k).wait_recv())
        mine[part(k)] = (
            buf[core, part(k)].astype(F32)
            + near[part(k)].astype(F32)
            + above[part(k)].astype(F32)
        ).astype(BF16)
        far_copy(k).start()

    def slab_sum(k):
        far_copy(k).wait_recv()
        plane[core, part(k)] = (
            mine[part(k)].astype(F32) + far[part(k)].astype(F32)
        ).astype(BF16)
        plane_copy(k).start()
        roll_own(k, 0)

    def mate_sum(k):
        plane_copy(k).wait_recv()
        roll_own(k, 1)

    def roll_own(k, p):
        where = (parts[p], part(k))
        own[where] = pltpu.roll(plane[where].astype(F32), shift, 1)

        @pl.when(jnp.logical_not(has_left) & has_right)
        def _():
            send_right[where] = own[where].astype(BF16)
            right_copy(k, p).start()

        @pl.when(jnp.logical_not(has_right) & has_left)
        def _():
            send_left[where] = own[where].astype(BF16)
            left_copy(k, p).start()

    def move_right(k, p):
        where = (parts[p], part(k))
        right_copy(k, p).wait_recv()

        @pl.when(has_right)
        def _():
            send_right[where] = (own[where] + wide(from_left, k, p)).astype(BF16)
            right_copy(k, p).start()

    def move_left(k, p):
        where = (parts[p], part(k))
        left_copy(k, p).wait_recv()

        @pl.when(has_left)
        def _():
            send_left[where] = (own[where] + wide(from_right, k, p)).astype(BF16)
            left_copy(k, p).start()

    def near_angles(k, p):
        pl.when(left_is_near & has_left)(lambda: move_right(k, p))
        pl.when(jnp.logical_not(left_is_near) & has_right)(lambda: move_left(k, p))

    def far_angles(k, p):
        pl.when(left_is_near & has_right)(lambda: move_left(k, p))
        pl.when(jnp.logical_not(left_is_near) & has_left)(lambda: move_right(k, p))
        total = own[parts[p], part(k)] + wide(from_left, k, p) + wide(from_right, k, p)
        out[parts[p], 0, part(k)] = (
            volume[parts[p], 0, part(k)].astype(F32) - step_size * total
        )

    def inside_far(k, p):
        pl.when(inside)(lambda: far_angles(k, p))

    stages = [
        (-3, start_near), (-1, lambda k: pl.when(has_next)(lambda: pass_below(k))),
        (0, pair_sum), (1, slab_sum), (2, mate_sum),
        (2, lambda k: near_angles(k, 0)), (3, lambda k: near_angles(k, 1)),
        (3, lambda k: inside_far(k, 0)), (4, lambda k: inside_far(k, 1)),
    ]
    for tick in range(-1, chunks + 4):
        for lag, stage in stages:
            if 0 <= tick - lag < chunks:
                stage(tick - lag)

    @pl.when(jnp.logical_not(inside))
    def _():
        for k in range(chunks):
            far_angles(k, 0)
            far_angles(k, 1)

    everything = pl.ds(0, rows)
    remote(buf.at[1 - core, everything], near, s2, r2.at[0], "slab", mate).wait_send()
    remote(mine, far, s4, r4.at[0], "slab", other).wait_send()
    remote(plane.at[core], plane.at[core], s5, r5.at[0], "slab", mate).wait_send()

    @pl.when(has_next)
    def _():
        remote(
            buf.at[1 - core, pl.ds(rows, rows)], near_below, s1, r1.at[0], "slab", mate
        ).wait_send()
        remote(below, above, s3, r3.at[0], "tile", tile + 1).wait_send()

    @pl.when(has_right)
    def _():
        remote(send_right, from_left, s6, r6.at[0, 0], "angle", angle + 1).wait_send()

    @pl.when(has_left)
    def _():
        remote(send_left, from_right, s7, r7.at[0, 0], "angle", angle - 1).wait_send()


def reduce_update(ids, volume, buf, tiles, angles, depth):
    rows, columns = volume.shape[2:]
    vmem = pl.BlockSpec(memory_space=pltpu.VMEM)
    dma = pltpu.SemaphoreType.DMA
    many = dma((rows // reduce_rows,))
    single = pltpu.VMEM((rows, columns), BF16)
    double = pltpu.VMEM((2, rows, columns), BF16)
    return pl.pallas_call(
        functools.partial(reduce_kernel, tiles, angles, depth),
        out_shape=jax.ShapeDtypeStruct(volume.shape, F32),
        in_specs=[pl.BlockSpec(memory_space=pltpu.SMEM), vmem, vmem],
        out_specs=vmem,
        scratch_shapes=[single] * 6
        + [double, pltpu.VMEM((2, rows, columns), F32)]
        + [double] * 4
        + [dma, many] * 5
        + [dma, dma((2, rows // reduce_rows))] * 2,
        compiler_params=pltpu.CompilerParams(
            collective_id=1, has_side_effects=True, vmem_limit_bytes=40 * MIB
        ),
    )(ids, volume, buf)


def per_device(tiles, angles, slabs, volume, probe, amplitudes, offsets, starts, counts, angle_ids):
    width = amplitudes.shape[-1]
    capacity = offsets.shape[3]
    depth = slabs * volume.shape[1]
    ext = project(angle_ids, volume, tiles, depth)
    buf = slots(
        offsets.reshape(capacity), starts.reshape(capacity), counts.reshape(1), ext, probe,
        amplitudes.reshape(capacity, width, width), dft_tables(width),
    )
    return reduce_update(angle_ids, volume, buf, tiles, angles, depth)


def solution(mesh):
    in_specs = (
        P(None, "slab", "tile", None),
        P(),
        P("angle", "tile", "slab", None, None, None),
        P("angle", "tile", "slab", None),
        P("angle", "tile", "slab", None),
        P("angle", "tile", "slab"),
        P("angle"),
    )
    body = functools.partial(
        per_device, mesh.shape["tile"], mesh.shape["angle"], mesh.shape["slab"]
    )
    return jax.shard_map(
        body, mesh=mesh, in_specs=in_specs, out_specs=P(None, "slab", "tile", None),
        check_vma=False,
    )
```
